32 devices in a mesh: groups: 2 (over y), dev: 2 (over core), side: 8 (over z, x).
Axes of the slice: x: 2, y: 2, z: 4, core: 2. Of those that a mesh axis runs over, the one named last changes fastest.
Arguments:
- queries: bfloat16 [4, 4, 8, 24, 128], P('groups', 'dev', 'side'), parts along dimension 0, may hold values from -2.5 to 2.5
- cache_keys: bfloat16 [4, 4, 8, 128, 4, 128], P('groups', 'dev', 'side'), parts along dimension 0, may hold values from -2.5 to 2.5
- cache_values: bfloat16 [4, 4, 8, 128, 4, 128], P('groups', 'dev', 'side'), parts along dimension 0, may hold values from -6 to 6
- new_keys: bfloat16 [4, 4, 8, 4, 128], P('groups', 'dev', 'side'), parts along dimension 0, may hold values from -2.5 to 2.5
- new_values: bfloat16 [4, 4, 8, 4, 128], P('groups', 'dev', 'side'), parts along dimension 0, may hold values from -6 to 6
- lengths: int32 [4, 4, 8], P('groups', 'dev', 'side'), parts along dimension 0, may hold values from 1 to 128, as said below
- out_weight: bfloat16 [3072, 3072], P(None, 'dev'), may hold values from -0.109375 to 0.109375
- residual: bfloat16 [4, 4, 8, 3072], P('groups', None, 'side', 'dev'), parts along dimension 0
- norm_gain: float32 [3072], replicated, may hold values from 0.1 to 1.9
- routes: int32 [4, 4, 8, 4], P('groups'), parts along dimension 0, may hold values from 0 to 7, all different within a row; in each aligned block of 16 rows (0 to 15, 16 to 31, ..., all dimensions but the last counted through in order) at most 9 rows name the same one
- route_probs: float32 [4, 4, 8, 4], P('groups', None, 'side'), parts along dimension 0, may hold values from 0.05 to 1
- w_gate: bfloat16 [8, 5376, 3072], P('side', 'dev'), may hold values from -0.109375 to 0.109375
- w_up: bfloat16 [8, 5376, 3072], P('side', 'dev'), may hold values from -0.109375 to 0.109375
- w_down: bfloat16 [8, 5376, 3072], P('side', 'dev'), may hold values from -0.078125 to 0.078125
Outputs:
- layer_out: bfloat16 [4, 4, 8, 3072], P('groups', None, 'side', 'dev'), parts along dimension 0
The draws below stay inside these ranges and needn't reach their ends.
There are 2 independent parts, one for each index of `groups`. The reference program is written for one: setup_inputs(seed, part) draws one part's arguments, and reference() takes and returns one part's arrays. A program takes and returns all parts, laid end to end along the dimension named above; an argument that names none is the same for every part. Nothing has to cross between parts.
Inputs may be any that keep to these rules, and one draw needn't show every extreme that they name: `routes`: each row names 4 different experts and every expert is named by some row; within one micro-batch the 16 rows held by one index of dev (aligned blocks in the order of the first three dimensions) name any one expert at most 9 times, and some block reaches 9. `lengths`: some row has 128 valid positions and some row has 1.
All inputs are finite; a program needn't handle non-finite values.
Results may differ from the reference program's by a relative error of at most 0.006.
Values may be sent and summed in bfloat16 or wider, within the bound.
No kernel may reach another device: no remote copies, remote signals or barrier semaphores. Data moves between devices by JAX's collectives and lax.ppermute only.
A program may use at most 128 MiB of HBM per device.

```python
import math
import jax
import jax.numpy as jnp
import numpy as np
from jax import lax

D = 3072
HEADS = 24
KV_HEADS = 4
HEAD_DIM = 128
FF = 5376
TOP = 4
MB = 2
CACHE = 128
EXPERTS = 8
ROWS_A = 4
BLOCK = 16
CAPG = 9
N_DEV = 2
N_SIDE = 8


def draw_lengths(key, part):
    key = jax.random.fold_in(key, 7)
    key_base, key_top, key_low = jax.random.split(key, 3)
    count_all = MB * ROWS_A * N_SIDE
    drawn = jax.random.randint(key_base, (count_all,), 1, CACHE + 1)
    top_at = jax.random.randint(key_top, (), 0, count_all)
    low_at = (top_at + jax.random.randint(key_low, (), 1, count_all)) % count_all
    places = jnp.arange(count_all)
    drawn = jnp.where(places == top_at, CACHE, drawn)
    drawn = jnp.where(places == low_at, 1, drawn)
    return drawn.reshape(MB, ROWS_A, N_SIDE).astype(jnp.int32)


def draw_residual(key, part):
    key = jax.random.fold_in(key, 11)
    key_cols, key_rows, key_vals = jax.random.split(key, 3)
    column_scale = jnp.exp(jax.random.uniform(key_cols, (D,), jnp.float32, math.log(0.3), math.log(3.0)))
    row_scale = jnp.exp(jax.random.uniform(key_rows, (MB, ROWS_A, N_SIDE, 1), jnp.float32, math.log(0.3), math.log(3.0)))
    values = jax.random.normal(key_vals, (MB, ROWS_A, N_SIDE, D), jnp.float32)
    return (values * column_scale * row_scale).astype(jnp.bfloat16)


def steps_of(rng, shape, cuts, smallest, largest):
    def one(dim, parts):
        draws = jax.random.uniform(jax.random.fold_in(jax.random.fold_in(rng, 6), dim), (parts,), jnp.float32, smallest / len(cuts), largest / len(cuts))
        return jnp.repeat(jnp.exp(draws), shape[dim] // parts).reshape((-1,) + (1,) * (len(shape) - dim - 1))

    level = one(*cuts[0])
    for cut in cuts[1:]:
        level = level * one(*cut)
    return level


def routed_block(stream_key, own, number, rows, count, top, most, skew):
    ranking = jax.random.permutation(stream_key, count)
    crowded, common = load_shares(count, rows * top, most, skew, True), load_shares(count, rows * top, most, skew, False)
    places = jnp.arange(count)

    def named(tallies, offset_by):
        used = int((tallies > 0).sum())
        fixed = max(1, used // 4)
        moved = fixed + (places - fixed + offset_by * (used - fixed)) % max(1, count - fixed)
        return jnp.zeros((count,), jnp.int32).at[ranking[jnp.where(places < fixed, places, moved)]].set(jnp.asarray(tallies, jnp.int32))

    tallies = jnp.where(number % 4 == 0, named(crowded, number // 4), named(common, number - number // 4 - 1))
    mixed = jax.random.permutation(jax.random.fold_in(own, 3), count)
    source_of, sink = mixed[0:count // 2 * 2:2], mixed[1:count // 2 * 2:2]
    margin = jnp.minimum(tallies[source_of] - 1, most - tallies[sink]) // 2
    margin = jnp.where((source_of == ranking[0]) | (sink == ranking[0]) | (tallies[sink] == 0), 0, jnp.maximum(margin, 0))
    moved = jax.random.randint(jax.random.fold_in(own, 4), (count // 2,), 0, 1 << 20) % (margin + 1)
    tallies = tallies.at[source_of].add(-moved).at[sink].add(moved)
    labels = jnp.searchsorted(jnp.cumsum(tallies), jnp.arange(rows * top), side="right").astype(jnp.int32)
    grid = labels.reshape(top, rows).T
    grid = grid[jax.random.permutation(jax.random.fold_in(own, 1), rows)]
    offset_by = jax.random.randint(jax.random.fold_in(own, 2), (rows, 1), 0, top)
    return jnp.take_along_axis(grid, (jnp.arange(top)[None, :] + offset_by) % top, axis=1)


def load_shares(amount, total, most, slope, full):
    loads = [(1 << 20) // math.isqrt(grade ** slope) + 1 for grade in range(1, amount + 1)]
    largest = most if full else min(most, max(-(-total // amount), total * loads[0] // sum(loads)))
    least = 1 if total - largest >= amount - 1 else 0
    holding, spare = [largest] + [least] * (amount - 1), total - largest - least * (amount - 1)
    while spare > 0:
        free = [i for i in range(1, amount) if holding[i] < largest] or [i for i in range(1, amount) if holding[i] < most]
        pool, remaining = sum([loads[i] for i in free]), spare
        for i in free:
            addition = min(most - holding[i], max(1, remaining * loads[i] // pool), spare)
            holding[i] = holding[i] + addition
            spare = spare - addition
    return np.array(holding)


def gaussian(rng, dims, scale, limit, cuts=(), kind=jnp.bfloat16):
    loudness = steps_of(rng, dims, cuts, -0.22, 0.18) if cuts else 1.0
    values = jax.random.normal(rng, dims, jnp.float32) * scale * loudness
    return jnp.minimum(jnp.maximum(values, -limit), limit).astype(kind)


def setup_inputs(seed: int = 0, part: int = 0) -> dict:
    key_list = jax.random.split(jax.random.key(seed), 15)
    own_keys = jax.random.split(jax.random.fold_in(key_list[14], part), 15)
    queries = gaussian(own_keys[0], (MB, ROWS_A, N_SIDE, HEADS, HEAD_DIM), 1.0, 2.5, ((1, 2), (2, 8)))
    cache_keys = gaussian(own_keys[1], (MB, ROWS_A, N_SIDE, CACHE, KV_HEADS, HEAD_DIM), 1.0, 2.5, ((1, 2), (2, 8)))
    cache_values = gaussian(own_keys[2], (MB, ROWS_A, N_SIDE, CACHE, KV_HEADS, HEAD_DIM), 1.0, 6.0, ((1, 2), (2, 8)))
    new_keys = gaussian(own_keys[3], (MB, ROWS_A, N_SIDE, KV_HEADS, HEAD_DIM), 1.0, 2.5, ((1, 2), (2, 8)))
    new_values = gaussian(own_keys[4], (MB, ROWS_A, N_SIDE, KV_HEADS, HEAD_DIM), 1.0, 6.0, ((1, 2), (2, 8)))
    lengths = draw_lengths(jax.random.fold_in(jax.random.fold_in(key_list[14], part), 71), part)
    out_weight = gaussian(key_list[6], (HEADS * HEAD_DIM, D), (HEADS * HEAD_DIM) ** -0.5, 0.109375, ((1, 2),))
    residual = draw_residual(jax.random.fold_in(jax.random.fold_in(key_list[14], part), 71), part)
    norm_gain = jnp.clip(1.0 + 0.18 * jax.random.normal(key_list[8], (D,), jnp.float32), 0.1, 1.9)
    routes_keys = jax.random.split(jax.random.fold_in(own_keys[9], 1), MB * ROWS_A * N_SIDE // BLOCK)
    routes_turns = jax.random.permutation(jax.random.fold_in(own_keys[9], 3), MB * ROWS_A * N_SIDE // BLOCK)
    routes = jax.vmap(lambda own, number: routed_block(jax.random.fold_in(own_keys[9], 2), own, number, BLOCK, EXPERTS, TOP, CAPG, 2))(routes_keys, routes_turns).reshape((MB, ROWS_A, N_SIDE, TOP))
    route_probs = jnp.clip(jnp.exp(math.log(1.0) - 2.9957323 * jax.random.uniform(own_keys[10], (MB, ROWS_A, N_SIDE, TOP), jnp.float32) ** steps_of(own_keys[10], (MB, ROWS_A, N_SIDE, TOP), ((2, 8),), -0.2, 0.2)), 0.05, 1.0)
    w_gate = gaussian(key_list[11], (EXPERTS, FF, D), D ** -0.5, 0.109375, ((0, 8), (1, 2)))
    w_up = gaussian(key_list[12], (EXPERTS, FF, D), D ** -0.5, 0.109375, ((0, 8), (1, 2)))
    w_down = gaussian(key_list[13], (EXPERTS, FF, D), FF ** -0.5, 0.078125, ((0, 8), (1, 2)))
    return dict(queries=queries, cache_keys=cache_keys, cache_values=cache_values, new_keys=new_keys, new_values=new_values, lengths=lengths, out_weight=out_weight, residual=residual, norm_gain=norm_gain, routes=routes, route_probs=route_probs, w_gate=w_gate, w_up=w_up, w_down=w_down)


norm_epsilon = 1e-05

def rounded(value):
    return lax.optimization_barrier(value.astype(jnp.bfloat16)).astype(jnp.float32)

def attend(queries, cache_keys, cache_values, new_keys, new_values, lengths):
    leading = queries.shape[:-2]
    head_count = queries.shape[-2]
    head_width = queries.shape[-1]
    key_heads = cache_keys.shape[-2]
    cache_size = cache_keys.shape[-3]
    grouped = queries.astype(jnp.float32).reshape(leading + (key_heads, head_count // key_heads, head_width))
    factor = 1.0 / math.sqrt(head_width)
    scores = jnp.einsum('...kgd,...ckd->...kgc', grouped, cache_keys.astype(jnp.float32), precision=lax.Precision.HIGHEST) * factor
    fresh = jnp.einsum('...kgd,...kd->...kg', grouped, new_keys.astype(jnp.float32), precision=lax.Precision.HIGHEST) * factor
    visible = jnp.arange(cache_size, dtype=jnp.int32) < lengths[..., None, None, None]
    raised = jnp.where(visible, jnp.exp(scores), 0.0)
    raised_new = jnp.exp(fresh)
    denominator = lax.optimization_barrier(jnp.sum(raised, axis=-1)) + raised_new
    weights = rounded(raised / denominator[..., None])
    weight_new = rounded(raised_new / denominator)
    mixed = jnp.einsum('...kgc,...ckd->...kgd', weights, cache_values.astype(jnp.float32), precision=lax.Precision.HIGHEST)
    mixed = mixed + weight_new[..., None] * new_values.astype(jnp.float32)[..., None, :]
    return mixed.astype(jnp.bfloat16).reshape(leading + (head_count * head_width,))

def normalize(values, scale_gain):
    widened = values.astype(jnp.float32)
    center = lax.optimization_barrier(jnp.mean(widened, axis=-1, keepdims=True))
    spread = lax.optimization_barrier(jnp.mean(jnp.square(widened - center), axis=-1, keepdims=True))
    return ((widened - center) * lax.rsqrt(spread + norm_epsilon) * scale_gain).astype(jnp.bfloat16)

def reference(queries, cache_keys, cache_values, new_keys, new_values, lengths, out_weight, residual, norm_gain, routes, route_probs, w_gate, w_up, w_down):
    attended = attend(queries, cache_keys, cache_values, new_keys, new_values, lengths)
    flattened = attended.reshape(-1, attended.shape[-1])
    projected = jnp.dot(flattened, out_weight, preferred_element_type=jnp.float32).astype(jnp.bfloat16).reshape(residual.shape)
    updated = (residual.astype(jnp.float32) + projected.astype(jnp.float32)).astype(jnp.bfloat16)
    normed = normalize(updated, norm_gain)
    gate_weights = route_probs / lax.optimization_barrier(jnp.sum(route_probs, axis=-1, keepdims=True))
    rows_total = residual.shape[1] * residual.shape[2]
    updated_rows = updated.reshape(MB, rows_total, D)
    normed_rows = normed.reshape(MB, rows_total, D)
    route_rows = routes.reshape(MB, rows_total, TOP)
    gate_rows = gate_weights.reshape(MB, rows_total, TOP)
    capacity_all = N_DEV * CAPG
    slice_width = FF // N_DEV
    outputs = []
    for batch_index in range(MB):
        rows_in = normed_rows[batch_index]
        row_picks = route_rows[batch_index]
        row_gates = gate_rows[batch_index]

        def expert_step(mixture, bundle):
            gate_matrix, up_matrix, down_matrix, expert_id = bundle
            routed = jnp.any(row_picks == expert_id, axis=-1)
            ordering = jnp.argsort(1 - routed.astype(jnp.int32), stable=True)[:capacity_all]
            chosen = rows_in[ordering]
            gate_part = jnp.dot(chosen, gate_matrix.T, preferred_element_type=jnp.float32)
            up_part = jnp.dot(chosen, up_matrix.T, preferred_element_type=jnp.float32)
            hidden = (jax.nn.silu(gate_part) * up_part).astype(jnp.bfloat16)

            def add_slice(slice_step, running):
                offset = (slice_step * slice_width).astype(jnp.int32)
                part_hidden = lax.dynamic_slice_in_dim(hidden, offset, slice_width, 1)
                part_down = lax.dynamic_slice_in_dim(down_matrix, offset, slice_width, 0)
                product = jnp.dot(part_hidden, part_down, preferred_element_type=jnp.float32)
                return running + rounded(product)
            summed = lax.fori_loop(0, N_DEV, add_slice, jnp.zeros((capacity_all, D), jnp.float32))
            result = rounded(summed)
            coefficient = lax.optimization_barrier(jnp.sum(row_gates * (row_picks == expert_id), axis=-1))[ordering]
            return (mixture.at[ordering].add(coefficient[:, None] * result), None)
        mixture, unused = lax.scan(expert_step, jnp.zeros((rows_total, D), jnp.float32), (w_gate, w_up, w_down, jnp.arange(EXPERTS, dtype=jnp.int32)))
        outputs.append((updated_rows[batch_index].astype(jnp.float32) + mixture).astype(jnp.bfloat16))
    return jnp.stack(outputs).reshape(residual.shape)
```

```python
import functools
import math

import jax
import jax.numpy as jnp
from jax import lax
from jax.experimental import pallas as pl
from jax.experimental.pallas import tpu as pltpu
from jax.sharding import PartitionSpec as P

norm_epsilon = 1e-05
vmem_bytes = 60 * 1024 * 1024
last_last = (((1,), (1,)), ((), ()))

smem_spec = pl.BlockSpec(memory_space=pltpu.SMEM)
vmem_spec = pl.BlockSpec(memory_space=pltpu.VMEM)


def attend_kernel(lengths, queries, keys, values, new_keys, new_values, out, scratch):
    row_count, head_count, head_width = queries.shape
    pair_count = keys.shape[1]
    key_heads = new_keys.shape[1]
    width = head_count // key_heads
    local_rows = lengths.shape[2]
    factor = 1.0 / math.sqrt(head_width)
    pair = lax.broadcasted_iota(jnp.int32, (head_count, pair_count), 1)
    head = lax.broadcasted_iota(jnp.int32, (head_count, pair_count), 0)
    own_key = (pair % key_heads) == (head // width)
    position = jnp.where(own_key, pair // key_heads, pair_count)
    key_head = lax.broadcasted_iota(jnp.int32, (head_count, head_width), 0) // width

    def spread(block):
        wide = block.astype(jnp.float32)
        result = jnp.zeros((head_count, head_width), jnp.float32)
        for index in range(key_heads):
            result = jnp.where(key_head == index, wide[index : index + 1, :], result)
        return result

    for row in range(row_count):
        query = queries[row]
        scores = (
            lax.dot_general(query, keys[row], last_last, preferred_element_type=jnp.float32)
            * factor
        )
        length = lengths[row // local_rows, 0, row % local_rows]
        raised = jnp.where(position < length, jnp.exp(scores), 0.0)
        fresh = (
            jnp.sum(query.astype(jnp.float32) * spread(new_keys[row]), axis=-1, keepdims=True)
            * factor
        )
        raised_new = jnp.exp(fresh)
        denominator = jnp.sum(raised, axis=-1, keepdims=True) + raised_new
        weights = (raised / denominator).astype(jnp.bfloat16)
        weight_new = (raised_new / denominator).astype(jnp.bfloat16).astype(jnp.float32)
        mixed = jnp.dot(weights, values[row], preferred_element_type=jnp.float32)
        mixed = mixed + weight_new * spread(new_values[row])
        scratch[pl.ds(row * head_count, head_count), :] = mixed
    pieces = [
        scratch[pl.ds(index, row_count, stride=head_count), :] for index in range(head_count)
    ]
    out[...] = jnp.concatenate(pieces, axis=1).astype(jnp.bfloat16)


def attend(queries, cache_keys, cache_values, new_keys, new_values, lengths):
    batch_count, local_rows = queries.shape[:2]
    rows = batch_count * local_rows
    head_count, head_width = queries.shape[-2:]
    key_heads = cache_keys.shape[-2]
    pairs = cache_keys.shape[-3] * key_heads
    return pl.pallas_call(
        attend_kernel,
        out_shape=jax.ShapeDtypeStruct((rows, head_count * head_width), jnp.bfloat16),
        in_specs=[smem_spec] + [vmem_spec] * 5,
        out_specs=vmem_spec,
        scratch_shapes=[pltpu.VMEM((rows * head_count, head_width), jnp.float32)],
        compiler_params=pltpu.CompilerParams(vmem_limit_bytes=vmem_bytes),
        name="attend",
    )(
        jnp.swapaxes(lengths, 1, 2),
        queries.reshape(rows, head_count, head_width),
        cache_keys.reshape(rows, pairs, head_width),
        cache_values.reshape(rows, pairs, head_width),
        new_keys.reshape(rows, key_heads, head_width),
        new_values.reshape(rows, key_heads, head_width),
    )


def halves(dev_index, own, other):
    first = jnp.where(dev_index == 0, own, other)
    second = jnp.where(dev_index == 0, other, own)
    return first, second


def project_kernel(dev_count, *refs):
    attended, (out_weight, residual, updated, copies, total) = refs[:-5], refs[-5:]
    batch_count, row_count, _ = residual.shape
    local_rows = row_count // dev_count
    step = pl.program_id(0)
    depth = out_weight.shape[0]
    columns = pl.ds(pl.multiple_of(step * depth, depth), depth)
    dev_index = lax.axis_index("dev")

    @pl.when(step == 0)
    def _():
        total[...] = jnp.zeros_like(total)

    parts = [ref[:, columns] for ref in attended]
    if len(parts) == 2:
        parts = [p.astype(jnp.float32) for p in parts]
        rows = jnp.concatenate(halves(dev_index, *parts), axis=0).astype(jnp.bfloat16)
    else:
        rows = parts[0]
    total[...] += jnp.dot(rows, out_weight[...], preferred_element_type=jnp.float32)

    @pl.when(step == pl.num_programs(0) - 1)
    def _():
        result = total[...]
        for batch in range(batch_count):
            pieces = []
            for dev in range(dev_count):
                start = (dev * batch_count + batch) * local_rows
                pieces.append(result[start : start + local_rows, :])
            projected = jnp.concatenate(pieces, axis=0).astype(jnp.bfloat16)
            rows = (
                residual[batch].astype(jnp.float32) + projected.astype(jnp.float32)
            ).astype(jnp.bfloat16)
            updated[batch] = rows
            for side in range(copies.shape[0]):
                copies[side, batch] = rows


def project(attended, out_weight, residual, dev_count, side_count):
    batch_count, row_count, width = residual.shape
    inner = out_weight.shape[0]
    depth = 512
    rows = batch_count * row_count
    return pl.pallas_call(
        functools.partial(project_kernel, dev_count),
        grid=(inner // depth,),
        out_shape=(
            jax.ShapeDtypeStruct((batch_count, row_count, width), jnp.bfloat16),
            jax.ShapeDtypeStruct((side_count, batch_count, row_count, width), jnp.bfloat16),
        ),
        in_specs=[pl.BlockSpec(part.shape, lambda k: (0, 0)) for part in attended]
        + [
            pl.BlockSpec((depth, width), lambda k: (k, 0)),
            pl.BlockSpec((batch_count, row_count, width), lambda k: (0, 0, 0)),
        ],
        out_specs=(
            pl.BlockSpec((batch_count, row_count, width), lambda k: (0, 0, 0)),
            pl.BlockSpec((side_count, batch_count, row_count, width), lambda k: (0, 0, 0, 0)),
        ),
        scratch_shapes=[pltpu.VMEM((rows, width), jnp.float32)],
        compiler_params=pltpu.CompilerParams(vmem_limit_bytes=vmem_bytes),
        name="project",
    )(*attended, out_weight, residual)


def expert_kernel(dev_count, part_count, *refs):
    parts, refs = refs[:part_count], refs[part_count:]
    gain, w_gate, w_up, w_down = refs[:4]
    outs, (normed, total) = refs[4:-2], refs[-2:]
    step = pl.program_id(1)
    dev_index = lax.axis_index("dev")

    @pl.when(step == 0)
    def _():
        wide = [part[...].astype(jnp.float32) for part in parts]
        if part_count == 2:
            wide = halves(dev_index, *wide)
        values = jnp.concatenate(wide, axis=1) if part_count > 1 else wide[0]
        center = jnp.mean(values, axis=-1, keepdims=True)
        values = values - center
        spread = jnp.mean(jnp.square(values), axis=-1, keepdims=True)
        normed[...] = (values * lax.rsqrt(spread + norm_epsilon) * gain[...]).astype(jnp.bfloat16)
        total[...] = jnp.zeros_like(total)

    rows = normed[...]
    gate = lax.dot_general(rows, w_gate[...], last_last, preferred_element_type=jnp.float32)
    up = lax.dot_general(rows, w_up[...], last_last, preferred_element_type=jnp.float32)
    hidden = (gate / (1.0 + jnp.exp(-gate)) * up).astype(jnp.bfloat16)
    total[...] += jnp.dot(hidden, w_down[...], preferred_element_type=jnp.float32)

    @pl.when(step == pl.num_programs(1) - 1)
    def _():
        if len(outs) == 2:
            half = total.shape[1] // 2
            low, high = total[:, :half], total[:, half:]
            outs[0][...] = jnp.where(dev_index == 0, low, high).astype(jnp.bfloat16)
            outs[1][...] = jnp.where(dev_index == 0, high, low).astype(jnp.bfloat16)
        else:
            outs[0][...] = total[...].astype(jnp.bfloat16)


def experts(parts, gain, w_gate, w_up, w_down, dev_count):
    rows = parts[0].shape[0]
    units, width = w_gate.shape
    block = min(rows, 128)
    chunk = 384 if units % 384 == 0 else units
    out_width = width // 2 if dev_count == 2 else width
    out_count = 2 if dev_count == 2 else 1
    return pl.pallas_call(
        functools.partial(expert_kernel, dev_count, len(parts)),
        grid=(rows // block, units // chunk),
        out_shape=[jax.ShapeDtypeStruct((rows, out_width), jnp.bfloat16)] * out_count,
        in_specs=[pl.BlockSpec((block, part.shape[1]), lambda r, f: (r, 0)) for part in parts]
        + [pl.BlockSpec((1, width), lambda r, f: (0, 0))]
        + [pl.BlockSpec((chunk, width), lambda r, f: (f, 0))] * 3,
        out_specs=[pl.BlockSpec((block, out_width), lambda r, f: (r, 0))] * out_count,
        scratch_shapes=[
            pltpu.VMEM((block, width), jnp.bfloat16),
            pltpu.VMEM((block, width), jnp.float32),
        ],
        compiler_params=pltpu.CompilerParams(vmem_limit_bytes=vmem_bytes),
        name="experts",
    )(*parts, gain.reshape(1, width), w_gate, w_up, w_down)


def combine_kernel(routes, probs, updated, returned, out):
    side_count = returned.shape[0]
    batch_count, row_count, width = updated.shape
    top_count = routes.shape[2]
    side_index = lax.axis_index("side")
    row_ids = lax.broadcasted_iota(jnp.int32, (row_count, 128), 0)
    lane_ids = lax.broadcasted_iota(jnp.int32, (row_count, 128), 1)
    for batch in range(batch_count):

        def place(row, shares):
            for top in range(top_count):
                expert = routes[batch, row, top, side_index]
                shares = jnp.where(
                    (row_ids == row) & (lane_ids == expert), probs[batch, row, 0, top], shares
                )
            return shares

        shares = jnp.zeros((row_count, 128), jnp.float32)
        if row_count <= 8:
            for row in range(row_count):
                shares = place(row, shares)
        else:
            shares = lax.fori_loop(0, row_count, place, shares)
        shares = shares / jnp.sum(shares, axis=-1, keepdims=True)
        mixture = jnp.zeros((row_count, width), jnp.float32)
        for expert in range(side_count):
            mixture = mixture + shares[:, expert : expert + 1] * returned[
                expert, batch
            ].astype(jnp.float32)
        out[batch] = (updated[batch].astype(jnp.float32) + mixture).astype(jnp.bfloat16)


def combine(routes, probs, updated, returned):
    return pl.pallas_call(
        combine_kernel,
        out_shape=jax.ShapeDtypeStruct(updated.shape, jnp.bfloat16),
        in_specs=[smem_spec, smem_spec, vmem_spec, vmem_spec],
        out_specs=vmem_spec,
        compiler_params=pltpu.CompilerParams(vmem_limit_bytes=vmem_bytes),
        name="combine",
    )(jnp.swapaxes(routes, 2, 3), probs, updated, returned)


def body(
    queries,
    cache_keys,
    cache_values,
    new_keys,
    new_values,
    lengths,
    out_weight,
    residual,
    norm_gain,
    routes,
    route_probs,
    w_gate,
    w_up,
    w_down,
):
    side_count = lax.axis_size("side")
    dev_count = lax.axis_size("dev")
    batch_count, row_count, _, column_width = residual.shape
    rows = batch_count * row_count
    swap = [(0, 1), (1, 0)]

    attended = attend(queries, cache_keys, cache_values, new_keys, new_values, lengths)
    if dev_count == 2:
        attended = (attended, lax.ppermute(attended, "dev", swap))
    else:
        attended = (lax.all_gather(attended, "dev", axis=0, tiled=True),)
    updated, copies = project(
        attended,
        out_weight,
        residual.reshape(batch_count, row_count, column_width),
        dev_count,
        side_count,
    )
    arrived = lax.all_to_all(copies, "side", split_axis=0, concat_axis=0, tiled=True)
    arrived = arrived.reshape(side_count * rows, column_width)
    if dev_count == 2:
        parts = (arrived, lax.ppermute(arrived, "dev", swap))
    else:
        parts = (lax.all_gather(arrived, "dev", axis=1, tiled=True),)
    sums = experts(parts, norm_gain, w_gate[0], w_up[0], w_down[0], dev_count)
    if dev_count == 2:
        own, given = sums
        total = own.astype(jnp.float32) + lax.ppermute(given, "dev", swap).astype(jnp.float32)
    else:
        pieces = sums[0].reshape(side_count * rows, dev_count, column_width)
        pieces = lax.all_to_all(pieces, "dev", split_axis=1, concat_axis=1, tiled=True)
        total = jnp.sum(pieces.astype(jnp.float32), axis=1)
    total = total.astype(jnp.bfloat16).reshape(side_count, batch_count, row_count, column_width)
    returned = lax.all_to_all(total, "side", split_axis=0, concat_axis=0, tiled=True)
    result = combine(routes, route_probs, updated, returned)
    return result.reshape(residual.shape)


def solution(mesh):
    placed = (
        P("groups", "dev", "side", None, None),
        P("groups", "dev", "side", None, None, None),
        P("groups", "dev", "side", None, None, None),
        P("groups", "dev", "side", None, None),
        P("groups", "dev", "side", None, None),
        P("groups", "dev", "side"),
        P(None, "dev"),
        P("groups", None, "side", "dev"),
        P(),
        P("groups", None, None, None),
        P("groups", None, "side", None),
        P("side", "dev", None),
        P("side", "dev", None),
        P("side", "dev", None),
    )
    return jax.shard_map(
        body,
        mesh=mesh,
        in_specs=placed,
        out_specs=P("groups", None, "side", "dev"),
        check_vma=False,
    )
```

```python
import functools
import math

import jax
import jax.numpy as jnp
from jax import lax
from jax.experimental import pallas as pl
from jax.experimental.pallas import tpu as pltpu
from jax.sharding import PartitionSpec as P

norm_epsilon = 1e-05
mebibyte = 1024 * 1024
hint_flops = 20_000_000_000
down_piece = 896
last_last = (((1,), (1,)), ((), ()))

smem_spec = pl.BlockSpec(memory_space=pltpu.SMEM)
vmem_spec = pl.BlockSpec(memory_space=pltpu.VMEM)


def attend_kernel(lengths, queries, keys, values, new_keys, new_values, out, scratch):
    row_count, head_count, head_width = queries.shape
    pair_count = keys.shape[1]
    key_heads = new_keys.shape[1]
    width = head_count // key_heads
    local_rows = lengths.shape[2]
    factor = 1.0 / math.sqrt(head_width)
    pair = lax.broadcasted_iota(jnp.int32, (head_count, pair_count), 1)
    head = lax.broadcasted_iota(jnp.int32, (head_count, pair_count), 0)
    own_key = (pair % key_heads) == (head // width)
    position = jnp.where(own_key, pair // key_heads, pair_count)
    key_head = lax.broadcasted_iota(jnp.int32, (head_count, head_width), 0) // width

    def spread(block):
        wide = block.astype(jnp.float32)
        result = jnp.zeros((head_count, head_width), jnp.float32)
        for index in range(key_heads):
            result = jnp.where(key_head == index, wide[index : index + 1, :], result)
        return result

    for row in range(row_count):
        query = queries[row]
        scores = (
            lax.dot_general(query, keys[row], last_last, preferred_element_type=jnp.float32)
            * factor
        )
        length = lengths[row // local_rows, 0, row % local_rows]
        raised = jnp.where(position < length, jnp.exp(scores), 0.0)
        fresh = (
            jnp.sum(query.astype(jnp.float32) * spread(new_keys[row]), axis=-1, keepdims=True)
            * factor
        )
        raised_new = jnp.exp(fresh)
        denominator = jnp.sum(raised, axis=-1, keepdims=True) + raised_new
        weights = (raised / denominator).astype(jnp.bfloat16)
        weight_new = (raised_new / denominator).astype(jnp.bfloat16).astype(jnp.float32)
        mixed = jnp.dot(weights, values[row], preferred_element_type=jnp.float32)
        mixed = mixed + weight_new * spread(new_values[row])
        scratch[pl.ds(row * head_count, head_count), :] = mixed
    pieces = [
        scratch[pl.ds(index, row_count, stride=head_count), :] for index in range(head_count)
    ]
    out[...] = jnp.concatenate(pieces, axis=1).astype(jnp.bfloat16)


def attend(queries, cache_keys, cache_values, new_keys, new_values, lengths):
    batch_count, local_rows = queries.shape[:2]
    rows = batch_count * local_rows
    head_count, head_width = queries.shape[-2:]
    key_heads = cache_keys.shape[-2]
    pairs = cache_keys.shape[-3] * key_heads
    return pl.pallas_call(
        attend_kernel,
        out_shape=jax.ShapeDtypeStruct((rows, head_count * head_width), jnp.bfloat16),
        in_specs=[smem_spec] + [vmem_spec] * 5,
        out_specs=vmem_spec,
        scratch_shapes=[pltpu.VMEM((rows * head_count, head_width), jnp.float32)],
        compiler_params=pltpu.CompilerParams(vmem_limit_bytes=8 * mebibyte),
        name="attend",
        cost_estimate=pl.CostEstimate(
            flops=hint_flops, transcendentals=0, bytes_accessed=cache_keys.size * 4
        ),
    )(
        jnp.swapaxes(lengths, 1, 2),
        queries.reshape(rows, head_count, head_width),
        cache_keys.reshape(rows, pairs, head_width),
        cache_values.reshape(rows, pairs, head_width),
        new_keys.reshape(rows, key_heads, head_width),
        new_values.reshape(rows, key_heads, head_width),
    )


def halves(dev_index, own, other):
    first = jnp.where(dev_index == 0, own, other)
    second = jnp.where(dev_index == 0, other, own)
    return first, second


def project_kernel(dev_count, *refs):
    attended, (out_weight, residual, updated, copies) = refs[:-4], refs[-4:]
    batch_count, row_count, _ = residual.shape
    local_rows = row_count // dev_count
    parts = [ref[...] for ref in attended]
    if len(parts) == 2:
        parts = [part.astype(jnp.float32) for part in parts]
        rows = jnp.concatenate(halves(lax.axis_index("dev"), *parts), axis=0).astype(jnp.bfloat16)
    else:
        rows = parts[0]
    result = jnp.dot(rows, out_weight[...], preferred_element_type=jnp.float32)
    whole = []
    for batch in range(batch_count):
        pieces = []
        for dev in range(dev_count):
            start = (dev * batch_count + batch) * local_rows
            pieces.append(result[start : start + local_rows, :])
        projected = jnp.concatenate(pieces, axis=0).astype(jnp.bfloat16)
        rows = (residual[batch].astype(jnp.float32) + projected.astype(jnp.float32)).astype(
            jnp.bfloat16
        )
        updated[batch] = rows
        whole.append(rows.astype(jnp.float32))
    whole = jnp.concatenate(whole, axis=0).astype(jnp.bfloat16)
    for side in range(copies.shape[0]):
        copies[side] = whole


def project(attended, out_weight, residual, dev_count, side_count):
    batch_count, row_count, width = residual.shape
    rows = batch_count * row_count
    return pl.pallas_call(
        functools.partial(project_kernel, dev_count),
        out_shape=(
            jax.ShapeDtypeStruct((batch_count, row_count, width), jnp.bfloat16),
            jax.ShapeDtypeStruct((side_count, rows, width), jnp.bfloat16),
        ),
        in_specs=[vmem_spec] * (len(attended) + 2),
        out_specs=(vmem_spec, vmem_spec),
        compiler_params=pltpu.CompilerParams(vmem_limit_bytes=4 * mebibyte),
        cost_estimate=pl.CostEstimate(
            flops=hint_flops, transcendentals=0, bytes_accessed=out_weight.size * 2
        ),
        name="project",
    )(*attended, pltpu.with_memory_space_constraint(out_weight, pltpu.VMEM), residual)


def pieces_of(length, piece):
    return [(start, min(piece, length - start)) for start in range(0, length, piece)]


def expert_kernel(dev_count, part_count, *refs):
    parts, refs = refs[:part_count], refs[part_count:]
    gain, w_gate, w_up, w_down = refs[:4]
    outs, (hidden, down, arrived) = refs[4:-3], refs[-3:]
    units, width = w_gate.shape
    dev_index = lax.axis_index("dev")
    copies = [
        pltpu.make_async_copy(
            w_down.at[pl.ds(start, size), :], down.at[pl.ds(start, size), :], arrived.at[index]
        )
        for index, (start, size) in enumerate(pieces_of(units, down_piece))
    ]

    @pl.when(pl.program_id(0) == 0)
    def _():
        for copy in copies:
            copy.start()

    wide = [part[...].astype(jnp.float32) for part in parts]
    if part_count == 2:
        wide = halves(dev_index, *wide)
    values = jnp.concatenate(wide, axis=1) if part_count > 1 else wide[0]
    center = jnp.mean(values, axis=-1, keepdims=True)
    values = values - center
    spread = jnp.mean(jnp.square(values), axis=-1, keepdims=True)
    rows = (values * lax.rsqrt(spread + norm_epsilon) * gain[...]).astype(jnp.bfloat16)
    for start, size in pieces_of(units, 512):
        span = slice(start, start + size)
        gate = lax.dot_general(rows, w_gate[span, :], last_last, preferred_element_type=jnp.float32)
        up = lax.dot_general(rows, w_up[span, :], last_last, preferred_element_type=jnp.float32)
        hidden[:, span] = (gate / (1.0 + jnp.exp(-gate)) * up).astype(jnp.bfloat16)

    @pl.when(pl.program_id(0) == 0)
    def _():
        for copy in copies:
            copy.wait()

    half = width // 2
    for start, size in pieces_of(half, 512):
        low = jnp.dot(
            hidden[...], down[:, start : start + size], preferred_element_type=jnp.float32
        )
        high = jnp.dot(
            hidden[...],
            down[:, half + start : half + start + size],
            preferred_element_type=jnp.float32,
        )
        if len(outs) == 2:
            span = slice(start, start + size)
            outs[0][:, span] = jnp.where(dev_index == 0, low, high).astype(jnp.bfloat16)
            outs[1][:, span] = jnp.where(dev_index == 0, high, low).astype(jnp.bfloat16)
        else:
            outs[0][:, start : start + size] = low.astype(jnp.bfloat16)
            outs[0][:, half + start : half + start + size] = high.astype(jnp.bfloat16)


def experts(parts, gain, w_gate, w_up, w_down, dev_count):
    rows = parts[0].shape[0]
    units, width = w_gate.shape
    block = min(rows, 128)
    out_width = width // 2 if dev_count == 2 else width
    out_count = 2 if dev_count == 2 else 1
    resident = functools.partial(pltpu.with_memory_space_constraint, memory_space=pltpu.VMEM)
    return pl.pallas_call(
        functools.partial(expert_kernel, dev_count, len(parts)),
        grid=(rows // block,),
        out_shape=[jax.ShapeDtypeStruct((rows, out_width), jnp.bfloat16)] * out_count,
        in_specs=[pl.BlockSpec((block, part.shape[1]), lambda r: (r, 0)) for part in parts]
        + [pl.BlockSpec((1, width), lambda r: (0, 0)), vmem_spec, vmem_spec]
        + [pl.BlockSpec(memory_space=pl.ANY)],
        out_specs=[pl.BlockSpec((block, out_width), lambda r: (r, 0))] * out_count,
        scratch_shapes=[
            pltpu.VMEM((block, units), jnp.bfloat16),
            pltpu.VMEM((units, width), jnp.bfloat16),
            pltpu.SemaphoreType.DMA((len(pieces_of(units, down_piece)),)),
        ],
        compiler_params=pltpu.CompilerParams(vmem_limit_bytes=19 * mebibyte),
        name="experts",
    )(*parts, gain.reshape(1, width), resident(w_gate), resident(w_up), w_down)


def combine_kernel(routes, probs, updated, returned, out):
    side_count = returned.shape[0]
    batch_count, row_count, width = updated.shape
    top_count = routes.shape[2]
    side_index = lax.axis_index("side")
    row_ids = lax.broadcasted_iota(jnp.int32, (row_count, 128), 0)
    lane_ids = lax.broadcasted_iota(jnp.int32, (row_count, 128), 1)
    for batch in range(batch_count):

        def place(row, shares):
            for top in range(top_count):
                expert = routes[batch, row, top, side_index]
                shares = jnp.where(
                    (row_ids == row) & (lane_ids == expert), probs[batch, row, 0, top], shares
                )
            return shares

        shares = jnp.zeros((row_count, 128), jnp.float32)
        if row_count <= 8:
            for row in range(row_count):
                shares = place(row, shares)
        else:
            shares = lax.fori_loop(0, row_count, place, shares)
        shares = shares / jnp.sum(shares, axis=-1, keepdims=True)
        mixture = jnp.zeros((row_count, width), jnp.float32)
        for expert in range(side_count):
            mixture = mixture + shares[:, expert : expert + 1] * returned[
                expert, batch
            ].astype(jnp.float32)
        out[batch] = (updated[batch].astype(jnp.float32) + mixture).astype(jnp.bfloat16)


def combine(routes, probs, updated, returned):
    return pl.pallas_call(
        combine_kernel,
        out_shape=jax.ShapeDtypeStruct(updated.shape, jnp.bfloat16),
        in_specs=[smem_spec, smem_spec, vmem_spec, vmem_spec],
        out_specs=vmem_spec,
        compiler_params=pltpu.CompilerParams(vmem_limit_bytes=8 * mebibyte),
        name="combine",
    )(jnp.swapaxes(routes, 2, 3), probs, updated, returned)


def body(
    queries,
    cache_keys,
    cache_values,
    new_keys,
    new_values,
    lengths,
    out_weight,
    residual,
    norm_gain,
    routes,
    route_probs,
    w_gate,
    w_up,
    w_down,
):
    side_count = lax.axis_size("side")
    dev_count = lax.axis_size("dev")
    batch_count, row_count, _, column_width = residual.shape
    rows = batch_count * row_count
    swap = [(0, 1), (1, 0)]

    attended = attend(queries, cache_keys, cache_values, new_keys, new_values, lengths)
    if dev_count == 2:
        attended = (attended, lax.ppermute(attended, "dev", swap))
    else:
        attended = (lax.all_gather(attended, "dev", axis=0, tiled=True),)
    updated, copies = project(
        attended,
        out_weight,
        residual.reshape(batch_count, row_count, column_width),
        dev_count,
        side_count,
    )
    arrived = lax.all_to_all(copies, "side", split_axis=0, concat_axis=0, tiled=True)
    arrived = arrived.reshape(side_count * rows, column_width)
    if dev_count == 2:
        parts = (arrived, lax.ppermute(arrived, "dev", swap))
    else:
        parts = (lax.all_gather(arrived, "dev", axis=1, tiled=True),)
    sums = experts(parts, norm_gain, w_gate[0], w_up[0], w_down[0], dev_count)
    if dev_count == 2:
        own, given = sums
        total = own.astype(jnp.float32) + lax.ppermute(given, "dev", swap).astype(jnp.float32)
    else:
        pieces = sums[0].reshape(side_count * rows, dev_count, column_width)
        pieces = lax.all_to_all(pieces, "dev", split_axis=1, concat_axis=1, tiled=True)
        total = jnp.sum(pieces.astype(jnp.float32), axis=1)
    total = total.astype(jnp.bfloat16).reshape(side_count, batch_count, row_count, column_width)
    returned = lax.all_to_all(total, "side", split_axis=0, concat_axis=0, tiled=True)
    result = combine(routes, route_probs, updated, returned)
    return result.reshape(residual.shape)


def solution(mesh):
    placed = (
        P("groups", "dev", "side", None, None),
        P("groups", "dev", "side", None, None, None),
        P("groups", "dev", "side", None, None, None),
        P("groups", "dev", "side", None, None),
        P("groups", "dev", "side", None, None),
        P("groups", "dev", "side"),
        P(None, "dev"),
        P("groups", None, "side", "dev"),
        P(),
        P("groups", None, None, None),
        P("groups", None, "side", None),
        P("side", "dev", None),
        P("side", "dev", None),
        P("side", "dev", None),
    )
    return jax.shard_map(
        body,
        mesh=mesh,
        in_specs=placed,
        out_specs=P("groups", None, "side", "dev"),
        check_vma=False,
    )
```

```python
import functools
import math

import jax
import jax.numpy as jnp
from jax import lax
from jax.experimental import pallas as pl
from jax.experimental.pallas import tpu as pltpu
from jax.sharding import PartitionSpec as P

norm_epsilon = 1e-05
mebibyte = 1024 * 1024
hint_flops = 20_000_000_000
down_piece = 896
last_last = (((1,), (1,)), ((), ()))

smem_spec = pl.BlockSpec(memory_space=pltpu.SMEM)
vmem_spec = pl.BlockSpec(memory_space=pltpu.VMEM)
in_hbm = functools.partial(pltpu.with_memory_space_constraint, memory_space=pltpu.HBM)
in_vmem = functools.partial(pltpu.with_memory_space_constraint, memory_space=pltpu.VMEM)


def share_rows(routes, probs, shares):
    batch_count, row_count, _ = shares.shape
    top_count = routes.shape[2]
    side_index = lax.axis_index("side")
    row_ids = lax.broadcasted_iota(jnp.int32, shares.shape[1:], 0)
    lane_ids = lax.broadcasted_iota(jnp.int32, shares.shape[1:], 1)
    for batch in range(batch_count):

        def place(row, placed):
            for top in range(top_count):
                expert = routes[batch, row, top, side_index]
                placed = jnp.where(
                    (row_ids == row) & (lane_ids == expert), probs[batch, row, 0, top], placed
                )
            return placed

        placed = jnp.zeros(shares.shape[1:], jnp.float32)
        if row_count <= 8:
            for row in range(row_count):
                placed = place(row, placed)
        else:
            placed = lax.fori_loop(0, row_count, place, placed)
        shares[batch] = placed / jnp.sum(placed, axis=-1, keepdims=True)


def attend_kernel(
    lengths, routes, probs, queries, keys, values, new_keys, new_values, out, shares, scratch
):
    row_count, head_count, head_width = queries.shape
    pair_count = keys.shape[1]
    key_heads = new_keys.shape[1]
    width = head_count // key_heads
    local_rows = lengths.shape[2]
    factor = 1.0 / math.sqrt(head_width)
    pair = lax.broadcasted_iota(jnp.int32, (head_count, pair_count), 1)
    head = lax.broadcasted_iota(jnp.int32, (head_count, pair_count), 0)
    own_key = (pair % key_heads) == (head // width)
    position = jnp.where(own_key, pair // key_heads, pair_count)
    key_head = lax.broadcasted_iota(jnp.int32, (head_count, head_width), 0) // width

    def spread(block):
        wide = block.astype(jnp.float32)
        result = jnp.zeros((head_count, head_width), jnp.float32)
        for index in range(key_heads):
            result = jnp.where(key_head == index, wide[index : index + 1, :], result)
        return result

    for row in range(row_count):
        query = queries[row]
        scores = (
            lax.dot_general(query, keys[row], last_last, preferred_element_type=jnp.float32)
            * factor
        )
        length = lengths[row // local_rows, 0, row % local_rows]
        raised = jnp.where(position < length, jnp.exp(scores), 0.0)
        fresh = (
            jnp.sum(query.astype(jnp.float32) * spread(new_keys[row]), axis=-1, keepdims=True)
            * factor
        )
        raised_new = jnp.exp(fresh)
        denominator = jnp.sum(raised, axis=-1, keepdims=True) + raised_new
        weights = (raised / denominator).astype(jnp.bfloat16)
        weight_new = (raised_new / denominator).astype(jnp.bfloat16).astype(jnp.float32)
        mixed = jnp.dot(weights, values[row], preferred_element_type=jnp.float32)
        mixed = mixed + weight_new * spread(new_values[row])
        scratch[pl.ds(row * head_count, head_count), :] = mixed
    pieces = [
        scratch[pl.ds(index, row_count, stride=head_count), :] for index in range(head_count)
    ]
    out[...] = jnp.concatenate(pieces, axis=1).astype(jnp.bfloat16)
    share_rows(routes, probs, shares)


def attend(queries, cache_keys, cache_values, new_keys, new_values, lengths, routes, probs):
    batch_count, local_rows = queries.shape[:2]
    rows = batch_count * local_rows
    head_count, head_width = queries.shape[-2:]
    key_heads = cache_keys.shape[-2]
    pairs = cache_keys.shape[-3] * key_heads
    return pl.pallas_call(
        attend_kernel,
        out_shape=(
            jax.ShapeDtypeStruct((rows, head_count * head_width), jnp.bfloat16),
            jax.ShapeDtypeStruct((batch_count, routes.shape[1], 128), jnp.float32),
        ),
        in_specs=[smem_spec] * 3 + [vmem_spec] * 5,
        out_specs=(vmem_spec, vmem_spec),
        scratch_shapes=[pltpu.VMEM((rows * head_count, head_width), jnp.float32)],
        compiler_params=pltpu.CompilerParams(vmem_limit_bytes=8 * mebibyte),
        name="attend",
        cost_estimate=pl.CostEstimate(
            flops=hint_flops, transcendentals=0, bytes_accessed=cache_keys.size * 4
        ),
    )(
        in_hbm(jnp.swapaxes(lengths, 1, 2)),
        in_hbm(jnp.swapaxes(routes, 2, 3)),
        in_hbm(probs),
        in_hbm(queries.reshape(rows, head_count, head_width)),
        in_hbm(cache_keys.reshape(rows, pairs, head_width)),
        in_hbm(cache_values.reshape(rows, pairs, head_width)),
        in_hbm(new_keys.reshape(rows, key_heads, head_width)),
        in_hbm(new_values.reshape(rows, key_heads, head_width)),
    )


def halves(dev_index, own, other):
    first = jnp.where(dev_index == 0, own, other)
    second = jnp.where(dev_index == 0, other, own)
    return first, second


def project_kernel(dev_count, *refs):
    attended, (out_weight, residual, updated, copies) = refs[:-4], refs[-4:]
    batch_count, row_count, _ = residual.shape
    local_rows = row_count // dev_count
    parts = [ref[...] for ref in attended]
    if len(parts) == 2:
        parts = [part.astype(jnp.float32) for part in parts]
        rows = jnp.concatenate(halves(lax.axis_index("dev"), *parts), axis=0).astype(jnp.bfloat16)
    else:
        rows = parts[0]
    result = jnp.dot(rows, out_weight[...], preferred_element_type=jnp.float32)
    whole = []
    for batch in range(batch_count):
        pieces = []
        for dev in range(dev_count):
            start = (dev * batch_count + batch) * local_rows
            pieces.append(result[start : start + local_rows, :])
        projected = jnp.concatenate(pieces, axis=0).astype(jnp.bfloat16)
        rows = (residual[batch].astype(jnp.float32) + projected.astype(jnp.float32)).astype(
            jnp.bfloat16
        )
        updated[batch] = rows
        whole.append(rows.astype(jnp.float32))
    whole = jnp.concatenate(whole, axis=0).astype(jnp.bfloat16)
    for side in range(copies.shape[0]):
        copies[side] = whole


def project(attended, out_weight, residual, dev_count, side_count):
    batch_count, row_count, width = residual.shape
    rows = batch_count * row_count
    return pl.pallas_call(
        functools.partial(project_kernel, dev_count),
        out_shape=(
            jax.ShapeDtypeStruct((batch_count, row_count, width), jnp.bfloat16),
            jax.ShapeDtypeStruct((side_count, rows, width), jnp.bfloat16),
        ),
        in_specs=[vmem_spec] * (len(attended) + 2),
        out_specs=(vmem_spec, vmem_spec),
        compiler_params=pltpu.CompilerParams(vmem_limit_bytes=4 * mebibyte),
        cost_estimate=pl.CostEstimate(
            flops=hint_flops, transcendentals=0, bytes_accessed=out_weight.size * 2
        ),
        name="project",
    )(*attended, in_vmem(out_weight), residual)


def pieces_of(length, piece):
    return [(start, min(piece, length - start)) for start in range(0, length, piece)]


def expert_kernel(dev_count, part_count, *refs):
    parts, refs = refs[:part_count], refs[part_count:]
    gain, w_gate, w_up, w_down = refs[:4]
    outs, (hidden, down, arrived) = refs[4:-3], refs[-3:]
    units, width = w_gate.shape
    dev_index = lax.axis_index("dev")
    copies = [
        pltpu.make_async_copy(
            w_down.at[pl.ds(start, size), :], down.at[pl.ds(start, size), :], arrived.at[index]
        )
        for index, (start, size) in enumerate(pieces_of(units, down_piece))
    ]

    @pl.when(pl.program_id(0) == 0)
    def _():
        for copy in copies:
            copy.start()

    wide = [part[...].astype(jnp.float32) for part in parts]
    if part_count == 2:
        wide = halves(dev_index, *wide)
    values = jnp.concatenate(wide, axis=1) if part_count > 1 else wide[0]
    center = jnp.mean(values, axis=-1, keepdims=True)
    values = values - center
    spread = jnp.mean(jnp.square(values), axis=-1, keepdims=True)
    rows = (values * lax.rsqrt(spread + norm_epsilon) * gain[...]).astype(jnp.bfloat16)
    @pl.when(dev_index < dev_count)
    def _():
        for start, size in pieces_of(units, 896):
            span = slice(start, start + size)
            gate = lax.dot_general(
                w_gate[span, :], rows, last_last, preferred_element_type=jnp.float32
            )
            up = lax.dot_general(w_up[span, :], rows, last_last, preferred_element_type=jnp.float32)
            hidden[:, span] = (gate / (1.0 + jnp.exp(-gate)) * up).T.astype(jnp.bfloat16)

    @pl.when(pl.program_id(0) == 0)
    def _():
        for copy in copies:
            copy.wait()

    half = width // 2
    for start, size in pieces_of(half, 512):
        low = jnp.dot(
            hidden[...], down[:, start : start + size], preferred_element_type=jnp.float32
        )
        high = jnp.dot(
            hidden[...],
            down[:, half + start : half + start + size],
            preferred_element_type=jnp.float32,
        )
        if len(outs) == 2:
            span = slice(start, start + size)
            outs[0][:, span] = jnp.where(dev_index == 0, low, high).astype(jnp.bfloat16)
            outs[1][:, span] = jnp.where(dev_index == 0, high, low).astype(jnp.bfloat16)
        else:
            outs[0][:, start : start + size] = low.astype(jnp.bfloat16)
            outs[0][:, half + start : half + start + size] = high.astype(jnp.bfloat16)


def experts(parts, gain, w_gate, w_up, w_down, dev_count):
    rows = parts[0].shape[0]
    units, width = w_gate.shape
    block = min(rows, 128)
    out_width = width // 2 if dev_count == 2 else width
    out_count = 2 if dev_count == 2 else 1
    return pl.pallas_call(
        functools.partial(expert_kernel, dev_count, len(parts)),
        grid=(rows // block,),
        out_shape=[jax.ShapeDtypeStruct((rows, out_width), jnp.bfloat16)] * out_count,
        in_specs=[pl.BlockSpec((block, part.shape[1]), lambda r: (r, 0)) for part in parts]
        + [pl.BlockSpec((1, width), lambda r: (0, 0)), vmem_spec, vmem_spec]
        + [pl.BlockSpec(memory_space=pl.ANY)],
        out_specs=[pl.BlockSpec((block, out_width), lambda r: (r, 0))] * out_count,
        scratch_shapes=[
            pltpu.VMEM((block, units), jnp.bfloat16),
            pltpu.VMEM((units, width), jnp.bfloat16),
            pltpu.SemaphoreType.DMA((len(pieces_of(units, down_piece)),)),
        ],
        compiler_params=pltpu.CompilerParams(vmem_limit_bytes=19 * mebibyte),
        name="experts",
    )(*parts, gain.reshape(1, width), in_vmem(w_gate), in_vmem(w_up), w_down)


def combine_kernel(shares, updated, returned, out):
    batch_count = updated.shape[0]
    for batch in range(batch_count):
        total = updated[batch].astype(jnp.float32)
        for expert in range(returned.shape[0]):
            share = shares[batch, :, expert : expert + 1]
            total = total + share * returned[expert, batch].astype(jnp.float32)
        out[batch] = total.astype(jnp.bfloat16)


def combine(shares, updated, returned):
    return pl.pallas_call(
        combine_kernel,
        out_shape=jax.ShapeDtypeStruct(updated.shape, jnp.bfloat16),
        in_specs=[vmem_spec] * 3,
        out_specs=vmem_spec,
        compiler_params=pltpu.CompilerParams(vmem_limit_bytes=8 * mebibyte),
        name="combine",
    )(shares, updated, returned)


def body(
    queries,
    cache_keys,
    cache_values,
    new_keys,
    new_values,
    lengths,
    out_weight,
    residual,
    norm_gain,
    routes,
    route_probs,
    w_gate,
    w_up,
    w_down,
):
    side_count = lax.axis_size("side")
    dev_count = lax.axis_size("dev")
    batch_count, row_count, _, column_width = residual.shape
    rows = batch_count * row_count
    swap = [(0, 1), (1, 0)]

    attended, shares = attend(
        queries, cache_keys, cache_values, new_keys, new_values, lengths, routes, route_probs
    )
    if dev_count == 2:
        attended = (attended, lax.ppermute(attended, "dev", swap))
    else:
        attended = (lax.all_gather(attended, "dev", axis=0, tiled=True),)
    updated, copies = project(
        attended,
        out_weight,
        residual.reshape(batch_count, row_count, column_width),
        dev_count,
        side_count,
    )
    arrived = lax.all_to_all(copies, "side", split_axis=0, concat_axis=0, tiled=True)
    arrived = arrived.reshape(side_count * rows, column_width)
    if dev_count == 2:
        parts = (arrived, lax.ppermute(arrived, "dev", swap))
    else:
        parts = (lax.all_gather(arrived, "dev", axis=1, tiled=True),)
    sums = experts(parts, norm_gain, w_gate[0], w_up[0], w_down[0], dev_count)
    if dev_count == 2:
        own, given = sums
        total = own.astype(jnp.float32) + lax.ppermute(given, "dev", swap).astype(jnp.float32)
    else:
        pieces = sums[0].reshape(side_count * rows, dev_count, column_width)
        pieces = lax.all_to_all(pieces, "dev", split_axis=1, concat_axis=1, tiled=True)
        total = jnp.sum(pieces.astype(jnp.float32), axis=1)
    total = total.astype(jnp.bfloat16).reshape(side_count, batch_count, row_count, column_width)
    returned = lax.all_to_all(total, "side", split_axis=0, concat_axis=0, tiled=True)
    result = combine(shares, updated, returned)
    return result.reshape(residual.shape)


def solution(mesh):
    placed = (
        P("groups", "dev", "side", None, None),
        P("groups", "dev", "side", None, None, None),
        P("groups", "dev", "side", None, None, None),
        P("groups", "dev", "side", None, None),
        P("groups", "dev", "side", None, None),
        P("groups", "dev", "side"),
        P(None, "dev"),
        P("groups", None, "side", "dev"),
        P(),
        P("groups", None, None, None),
        P("groups", None, "side", None),
        P("side", "dev", None),
        P("side", "dev", None),
        P("side", "dev", None),
    )
    return jax.shard_map(
        body,
        mesh=mesh,
        in_specs=placed,
        out_specs=P("groups", None, "side", "dev"),
        check_vma=False,
    )
```

```python
import functools
import math

import jax
import jax.numpy as jnp
from jax import lax
from jax.experimental import pallas as pl
from jax.experimental.pallas import tpu as pltpu
from jax.sharding import PartitionSpec as P

norm_epsilon = 1e-05
mebibyte = 1024 * 1024
hint_flops = 20_000_000_000
last_last = (((1,), (1,)), ((), ()))

smem_spec = pl.BlockSpec(memory_space=pltpu.SMEM)
vmem_spec = pl.BlockSpec(memory_space=pltpu.VMEM)
in_hbm = functools.partial(pltpu.with_memory_space_constraint, memory_space=pltpu.HBM)
in_vmem = functools.partial(pltpu.with_memory_space_constraint, memory_space=pltpu.VMEM)


def share_rows(routes, probs, shares):
    batch_count, row_count, _ = shares.shape
    top_count = routes.shape[2]
    side_index = lax.axis_index("side")
    row_ids = lax.broadcasted_iota(jnp.int32, shares.shape[1:], 0)
    lane_ids = lax.broadcasted_iota(jnp.int32, shares.shape[1:], 1)
    for batch in range(batch_count):

        def place(row, placed):
            for top in range(top_count):
                expert = routes[batch, row, top, side_index]
                placed = jnp.where(
                    (row_ids == row) & (lane_ids == expert), probs[batch, row, 0, top], placed
                )
            return placed

        placed = jnp.zeros(shares.shape[1:], jnp.float32)
        if row_count <= 8:
            for row in range(row_count):
                placed = place(row, placed)
        else:
            placed = lax.fori_loop(0, row_count, place, placed)
        shares[batch] = placed / jnp.sum(placed, axis=-1, keepdims=True)


def attend_kernel(
    lengths, routes, probs, queries, keys, values, new_keys, new_values, out, shares, scratch
):
    row_count, head_count, head_width = queries.shape
    pair_count = keys.shape[1]
    key_heads = new_keys.shape[1]
    width = head_count // key_heads
    local_rows = lengths.shape[2]
    factor = 1.0 / math.sqrt(head_width)
    pair = lax.broadcasted_iota(jnp.int32, (head_count, pair_count), 1)
    head = lax.broadcasted_iota(jnp.int32, (head_count, pair_count), 0)
    own_key = (pair % key_heads) == (head // width)
    position = jnp.where(own_key, pair // key_heads, pair_count)
    key_head = lax.broadcasted_iota(jnp.int32, (head_count, head_width), 0) // width

    def spread(block):
        wide = block.astype(jnp.float32)
        result = jnp.zeros((head_count, head_width), jnp.float32)
        for index in range(key_heads):
            result = jnp.where(key_head == index, wide[index : index + 1, :], result)
        return result

    for row in range(row_count):
        query = queries[row]
        scores = (
            lax.dot_general(query, keys[row], last_last, preferred_element_type=jnp.float32)
            * factor
        )
        length = lengths[row // local_rows, 0, row % local_rows]
        raised = jnp.where(position < length, jnp.exp(scores), 0.0)
        fresh = (
            jnp.sum(query.astype(jnp.float32) * spread(new_keys[row]), axis=-1, keepdims=True)
            * factor
        )
        raised_new = jnp.exp(fresh)
        denominator = jnp.sum(raised, axis=-1, keepdims=True) + raised_new
        weights = (raised / denominator).astype(jnp.bfloat16)
        weight_new = (raised_new / denominator).astype(jnp.bfloat16).astype(jnp.float32)
        mixed = jnp.dot(weights, values[row], preferred_element_type=jnp.float32)
        mixed = mixed + weight_new * spread(new_values[row])
        scratch[pl.ds(row * head_count, head_count), :] = mixed
    pieces = [
        scratch[pl.ds(index, row_count, stride=head_count), :] for index in range(head_count)
    ]
    out[...] = jnp.concatenate(pieces, axis=1).astype(jnp.bfloat16)
    share_rows(routes, probs, shares)


def attend(queries, cache_keys, cache_values, new_keys, new_values, lengths, routes, probs):
    batch_count, local_rows = queries.shape[:2]
    rows = batch_count * local_rows
    head_count, head_width = queries.shape[-2:]
    key_heads = cache_keys.shape[-2]
    pairs = cache_keys.shape[-3] * key_heads
    return pl.pallas_call(
        attend_kernel,
        out_shape=(
            jax.ShapeDtypeStruct((rows, head_count * head_width), jnp.bfloat16),
            jax.ShapeDtypeStruct((batch_count, routes.shape[1], 128), jnp.float32),
        ),
        in_specs=[smem_spec] * 3 + [vmem_spec] * 5,
        out_specs=(vmem_spec, vmem_spec),
        scratch_shapes=[pltpu.VMEM((rows * head_count, head_width), jnp.float32)],
        compiler_params=pltpu.CompilerParams(vmem_limit_bytes=3 * mebibyte),
        name="attend",
        cost_estimate=pl.CostEstimate(
            flops=hint_flops, transcendentals=0, bytes_accessed=cache_keys.size * 4
        ),
    )(
        in_hbm(jnp.swapaxes(lengths, 1, 2)),
        in_hbm(jnp.swapaxes(routes, 2, 3)),
        in_hbm(probs),
        in_hbm(queries.reshape(rows, head_count, head_width)),
        in_hbm(cache_keys.reshape(rows, pairs, head_width)),
        in_hbm(cache_values.reshape(rows, pairs, head_width)),
        in_hbm(new_keys.reshape(rows, key_heads, head_width)),
        in_hbm(new_values.reshape(rows, key_heads, head_width)),
    )


def halves(dev_index, own, other):
    first = jnp.where(dev_index == 0, own, other)
    second = jnp.where(dev_index == 0, other, own)
    return first, second


def project_kernel(dev_count, *refs):
    attended, (out_weight, residual, updated, copies) = refs[:-4], refs[-4:]
    batch_count, row_count, _ = residual.shape
    local_rows = row_count // dev_count
    parts = [ref[...] for ref in attended]
    if len(parts) == 2:
        parts = [part.astype(jnp.float32) for part in parts]
        rows = jnp.concatenate(halves(lax.axis_index("dev"), *parts), axis=0).astype(jnp.bfloat16)
    else:
        rows = parts[0]
    result = jnp.dot(rows, out_weight[...], preferred_element_type=jnp.float32)
    whole = []
    for batch in range(batch_count):
        pieces = []
        for dev in range(dev_count):
            start = (dev * batch_count + batch) * local_rows
            pieces.append(result[start : start + local_rows, :])
        projected = jnp.concatenate(pieces, axis=0).astype(jnp.bfloat16)
        rows = (residual[batch].astype(jnp.float32) + projected.astype(jnp.float32)).astype(
            jnp.bfloat16
        )
        updated[batch] = rows
        whole.append(rows.astype(jnp.float32))
    whole = jnp.concatenate(whole, axis=0).astype(jnp.bfloat16)
    for side in range(copies.shape[0]):
        copies[side] = whole


def project(attended, out_weight, residual, dev_count, side_count):
    batch_count, row_count, width = residual.shape
    rows = batch_count * row_count
    return pl.pallas_call(
        functools.partial(project_kernel, dev_count),
        out_shape=(
            jax.ShapeDtypeStruct((batch_count, row_count, width), jnp.bfloat16),
            jax.ShapeDtypeStruct((side_count, rows, width), jnp.bfloat16),
        ),
        in_specs=[vmem_spec] * (len(attended) + 2),
        out_specs=(vmem_spec, vmem_spec),
        compiler_params=pltpu.CompilerParams(vmem_limit_bytes=2 * mebibyte),
        cost_estimate=pl.CostEstimate(
            flops=hint_flops, transcendentals=0, bytes_accessed=out_weight.size * 2
        ),
        name="project",
    )(*attended, in_vmem(out_weight), residual)


def pieces_of(length, piece):
    return [(start, min(piece, length - start)) for start in range(0, length, piece)]


def normalize(parts, gain):
    width = sum(part.shape[1] for part in parts)
    center = sum(jnp.sum(part, axis=-1, keepdims=True) for part in parts) / width
    parts = [part - center for part in parts]
    spread = sum(jnp.sum(jnp.square(part), axis=-1, keepdims=True) for part in parts) / width
    values = jnp.concatenate(parts, axis=1) if len(parts) > 1 else parts[0]
    return (values * lax.rsqrt(spread + norm_epsilon) * gain).astype(jnp.bfloat16)


def hidden_rows(parts, gain, w_gate, w_up, hidden):
    rows = normalize(parts, gain[...])
    for start, size in pieces_of(w_gate.shape[0], 896):
        span = slice(start, start + size)
        gate = lax.dot_general(w_gate[span, :], rows, last_last, preferred_element_type=jnp.float32)
        up = lax.dot_general(w_up[span, :], rows, last_last, preferred_element_type=jnp.float32)
        hidden[:, span] = (gate / (1.0 + jnp.exp(-gate)) * up).T.astype(jnp.bfloat16)


def pair_kernel(own, other, gain, w_gate, w_up, w_down, hidden, given, kept, lent, arrived):
    dev_index = lax.axis_index("dev")
    width = own.shape[1]
    copies = [
        pltpu.make_async_copy(
            w_down.at[:, pl.ds(pl.multiple_of(dev * width, width), width)],
            target,
            arrived.at[index],
        )
        for index, (dev, target) in enumerate(((1 - dev_index, lent), (dev_index, kept)))
    ]
    for copy in copies:
        copy.start()

    @pl.when(dev_index < 2)
    def _():
        parts = halves(dev_index, own[...].astype(jnp.float32), other[...].astype(jnp.float32))
        hidden_rows(parts, gain, w_gate, w_up, hidden)

    for copy in copies:
        copy.wait()
    given[...] = jnp.dot(hidden[...], lent[...], preferred_element_type=jnp.float32).astype(
        jnp.bfloat16
    )


def down_kernel(hidden, kept, out):
    out[...] = jnp.dot(hidden[...], kept[...], preferred_element_type=jnp.float32).astype(
        jnp.bfloat16
    )


def pair_experts(arrived, gain, w_gate, w_up, w_down):
    swap = [(0, 1), (1, 0)]
    rows, half = arrived.shape
    units, width = w_gate.shape
    hidden, given, kept = pl.pallas_call(
        pair_kernel,
        out_shape=(
            jax.ShapeDtypeStruct((rows, units), jnp.bfloat16),
            jax.ShapeDtypeStruct((rows, half), jnp.bfloat16),
            pltpu.VMEM((units, half), jnp.bfloat16),
        ),
        in_specs=[vmem_spec] * 5 + [pl.BlockSpec(memory_space=pl.ANY)],
        out_specs=(vmem_spec,) * 3,
        scratch_shapes=[
            pltpu.VMEM((units, half), jnp.bfloat16),
            pltpu.SemaphoreType.DMA((2,)),
        ],
        compiler_params=pltpu.CompilerParams(vmem_limit_bytes=12 * mebibyte),
        name="experts",
    )(
        arrived,
        lax.ppermute(arrived, "dev", swap),
        gain.reshape(1, width),
        in_vmem(w_gate),
        in_vmem(w_up),
        in_hbm(w_down),
    )
    taken = lax.ppermute(given, "dev", swap)
    own = pl.pallas_call(
        down_kernel,
        out_shape=jax.ShapeDtypeStruct((rows, half), jnp.bfloat16),
        in_specs=[vmem_spec, vmem_spec],
        out_specs=vmem_spec,
        compiler_params=pltpu.CompilerParams(vmem_limit_bytes=2 * mebibyte),
        name="down_own",
    )(hidden, in_vmem(kept))
    return own.astype(jnp.float32) + taken.astype(jnp.float32)


def whole_kernel(rows, gain, w_gate, w_up, w_down, out, hidden):
    hidden_rows([rows[...].astype(jnp.float32)], gain, w_gate, w_up, hidden)
    out[...] = jnp.dot(hidden[...], w_down[...], preferred_element_type=jnp.float32).astype(
        jnp.bfloat16
    )


def whole_experts(arrived, gain, w_gate, w_up, w_down):
    rows, part_width = arrived.shape
    units, width = w_gate.shape
    block = min(rows, 128)
    gathered = lax.all_gather(arrived, "dev", axis=1, tiled=True)
    given = pl.pallas_call(
        whole_kernel,
        grid=(rows // block,),
        out_shape=jax.ShapeDtypeStruct((rows, width), jnp.bfloat16),
        in_specs=[pl.BlockSpec((block, width), lambda r: (r, 0))]
        + [pl.BlockSpec((1, width), lambda r: (0, 0)), vmem_spec, vmem_spec, vmem_spec],
        out_specs=pl.BlockSpec((block, width), lambda r: (r, 0)),
        scratch_shapes=[pltpu.VMEM((block, units), jnp.bfloat16)],
        compiler_params=pltpu.CompilerParams(vmem_limit_bytes=24 * mebibyte),
        name="experts",
    )(gathered, gain.reshape(1, width), w_gate, w_up, w_down)
    pieces = given.reshape(rows, width // part_width, part_width)
    pieces = lax.all_to_all(pieces, "dev", split_axis=1, concat_axis=1, tiled=True)
    return jnp.sum(pieces.astype(jnp.float32), axis=1)


def combine_kernel(shares, updated, returned, out):
    batch_count = updated.shape[0]
    for batch in range(batch_count):
        total = updated[batch].astype(jnp.float32)
        for expert in range(returned.shape[0]):
            share = shares[batch, :, expert : expert + 1]
            total = total + share * returned[expert, batch].astype(jnp.float32)
        out[batch] = total.astype(jnp.bfloat16)


def combine(shares, updated, returned):
    return pl.pallas_call(
        combine_kernel,
        out_shape=jax.ShapeDtypeStruct(updated.shape, jnp.bfloat16),
        in_specs=[vmem_spec] * 3,
        out_specs=vmem_spec,
        compiler_params=pltpu.CompilerParams(vmem_limit_bytes=8 * mebibyte),
        name="combine",
    )(shares, updated, returned)


def body(
    queries,
    cache_keys,
    cache_values,
    new_keys,
    new_values,
    lengths,
    out_weight,
    residual,
    norm_gain,
    routes,
    route_probs,
    w_gate,
    w_up,
    w_down,
):
    side_count = lax.axis_size("side")
    dev_count = lax.axis_size("dev")
    batch_count, row_count, _, column_width = residual.shape
    rows = batch_count * row_count
    swap = [(0, 1), (1, 0)]

    attended, shares = attend(
        queries, cache_keys, cache_values, new_keys, new_values, lengths, routes, route_probs
    )
    if dev_count == 2:
        attended = (attended, lax.ppermute(attended, "dev", swap))
    else:
        attended = (lax.all_gather(attended, "dev", axis=0, tiled=True),)
    updated, copies = project(
        attended,
        out_weight,
        residual.reshape(batch_count, row_count, column_width),
        dev_count,
        side_count,
    )
    arrived = lax.all_to_all(copies, "side", split_axis=0, concat_axis=0, tiled=True)
    arrived = arrived.reshape(side_count * rows, column_width)
    gather_and_run = pair_experts if dev_count == 2 else whole_experts
    total = gather_and_run(arrived, norm_gain, w_gate[0], w_up[0], w_down[0])
    total = total.astype(jnp.bfloat16).reshape(side_count, batch_count, row_count, column_width)
    returned = lax.all_to_all(total, "side", split_axis=0, concat_axis=0, tiled=True)
    result = combine(shares, updated, returned)
    return result.reshape(residual.shape)


def solution(mesh):
    placed = (
        P("groups", "dev", "side", None, None),
        P("groups", "dev", "side", None, None, None),
        P("groups", "dev", "side", None, None, None),
        P("groups", "dev", "side", None, None),
        P("groups", "dev", "side", None, None),
        P("groups", "dev", "side"),
        P(None, "dev"),
        P("groups", None, "side", "dev"),
        P(),
        P("groups", None, None, None),
        P("groups", None, "side", None),
        P("side", "dev", None),
        P("side", "dev", None),
        P("side", "dev", None),
    )
    return jax.shard_map(
        body,
        mesh=mesh,
        in_specs=placed,
        out_specs=P("groups", None, "side", "dev"),
        check_vma=False,
    )
```

```python
import functools
import math

import jax
import jax.numpy as jnp
from jax import lax
from jax.experimental import pallas as pl
from jax.experimental.pallas import tpu as pltpu
from jax.sharding import PartitionSpec as P

norm_epsilon = 1e-05
mebibyte = 1024 * 1024
mxu_count, mxu_size = 2, 256
hint_flops = 20_000_000_000
last_last = (((1,), (1,)), ((), ()))

smem_spec = pl.BlockSpec(memory_space=pltpu.SMEM)
vmem_spec = pl.BlockSpec(memory_space=pltpu.VMEM)
in_hbm = functools.partial(pltpu.with_memory_space_constraint, memory_space=pltpu.HBM)
in_vmem = functools.partial(pltpu.with_memory_space_constraint, memory_space=pltpu.VMEM)


def share_rows(routes, probs, shares):
    batch_count, row_count, _ = shares.shape
    top_count = routes.shape[2]
    side_index = lax.axis_index("side")
    row_ids = lax.broadcasted_iota(jnp.int32, shares.shape[1:], 0)
    lane_ids = lax.broadcasted_iota(jnp.int32, shares.shape[1:], 1)
    for batch in range(batch_count):

        def place(row, placed):
            for top in range(top_count):
                expert = routes[batch, row, top, side_index]
                placed = jnp.where(
                    (row_ids == row) & (lane_ids == expert), probs[batch, row, 0, top], placed
                )
            return placed

        placed = jnp.zeros(shares.shape[1:], jnp.float32)
        if row_count <= 8:
            for row in range(row_count):
                placed = place(row, placed)
        else:
            placed = lax.fori_loop(0, row_count, place, placed)
        shares[batch] = placed / jnp.sum(placed, axis=-1, keepdims=True)


def attend_kernel(
    lengths, routes, probs, queries, keys, values, new_keys, new_values, out, shares, scratch
):
    row_count, head_count, head_width = queries.shape
    pair_count = keys.shape[1]
    key_heads = new_keys.shape[1]
    width = head_count // key_heads
    local_rows = lengths.shape[2]
    factor = 1.0 / math.sqrt(head_width)
    pair = lax.broadcasted_iota(jnp.int32, (head_count, pair_count), 1)
    head = lax.broadcasted_iota(jnp.int32, (head_count, pair_count), 0)
    own_key = (pair % key_heads) == (head // width)
    position = jnp.where(own_key, pair // key_heads, pair_count)
    key_head = lax.broadcasted_iota(jnp.int32, (head_count, head_width), 0) // width

    def spread(block):
        wide = block.astype(jnp.float32)
        result = jnp.zeros((head_count, head_width), jnp.float32)
        for index in range(key_heads):
            result = jnp.where(key_head == index, wide[index : index + 1, :], result)
        return result

    for row in range(row_count):
        query = queries[row]
        scores = (
            lax.dot_general(query, keys[row], last_last, preferred_element_type=jnp.float32)
            * factor
        )
        length = lengths[row // local_rows, 0, row % local_rows]
        raised = jnp.where(position < length, jnp.exp(scores), 0.0)
        fresh = (
            jnp.sum(query.astype(jnp.float32) * spread(new_keys[row]), axis=-1, keepdims=True)
            * factor
        )
        raised_new = jnp.exp(fresh)
        denominator = jnp.sum(raised, axis=-1, keepdims=True) + raised_new
        weights = (raised / denominator).astype(jnp.bfloat16)
        weight_new = (raised_new / denominator).astype(jnp.bfloat16).astype(jnp.float32)
        mixed = jnp.dot(weights, values[row], preferred_element_type=jnp.float32)
        mixed = mixed + weight_new * spread(new_values[row])
        scratch[pl.ds(row * head_count, head_count), :] = mixed
    pieces = [
        scratch[pl.ds(index, row_count, stride=head_count), :] for index in range(head_count)
    ]
    out[...] = jnp.concatenate(pieces, axis=1).astype(jnp.bfloat16)
    share_rows(routes, probs, shares)


def attend(queries, cache_keys, cache_values, new_keys, new_values, lengths, routes, probs):
    batch_count, local_rows = queries.shape[:2]
    rows = batch_count * local_rows
    head_count, head_width = queries.shape[-2:]
    key_heads = cache_keys.shape[-2]
    pairs = cache_keys.shape[-3] * key_heads
    return pl.pallas_call(
        attend_kernel,
        out_shape=(
            jax.ShapeDtypeStruct((rows, head_count * head_width), jnp.bfloat16),
            jax.ShapeDtypeStruct((batch_count, routes.shape[1], 128), jnp.float32),
        ),
        in_specs=[smem_spec] * 3 + [vmem_spec] * 5,
        out_specs=(vmem_spec, vmem_spec),
        scratch_shapes=[pltpu.VMEM((rows * head_count, head_width), jnp.float32)],
        compiler_params=pltpu.CompilerParams(vmem_limit_bytes=3 * mebibyte),
        name="attend",
        cost_estimate=pl.CostEstimate(
            flops=hint_flops, transcendentals=0, bytes_accessed=cache_keys.size * 4
        ),
    )(
        in_hbm(jnp.swapaxes(lengths, 1, 2)),
        in_hbm(jnp.swapaxes(routes, 2, 3)),
        in_hbm(probs),
        in_hbm(queries.reshape(rows, head_count, head_width)),
        in_hbm(cache_keys.reshape(rows, pairs, head_width)),
        in_hbm(cache_values.reshape(rows, pairs, head_width)),
        in_hbm(new_keys.reshape(rows, key_heads, head_width)),
        in_hbm(new_values.reshape(rows, key_heads, head_width)),
    )


def halves(dev_index, own, other):
    first = jnp.where(dev_index == 0, own, other)
    second = jnp.where(dev_index == 0, other, own)
    return first, second


def project_kernel(dev_count, *refs):
    attended, (out_weight, residual, updated, copies) = refs[:-4], refs[-4:]
    batch_count, row_count, _ = residual.shape
    local_rows = row_count // dev_count
    parts = [ref[...] for ref in attended]
    if len(parts) == 2:
        parts = [part.astype(jnp.float32) for part in parts]
        rows = jnp.concatenate(halves(lax.axis_index("dev"), *parts), axis=0).astype(jnp.bfloat16)
    else:
        rows = parts[0]
    result = jnp.dot(rows, out_weight[...], preferred_element_type=jnp.float32)
    whole = []
    for batch in range(batch_count):
        pieces = []
        for dev in range(dev_count):
            start = (dev * batch_count + batch) * local_rows
            pieces.append(result[start : start + local_rows, :])
        projected = jnp.concatenate(pieces, axis=0).astype(jnp.bfloat16)
        rows = (residual[batch].astype(jnp.float32) + projected.astype(jnp.float32)).astype(
            jnp.bfloat16
        )
        updated[batch] = rows
        whole.append(rows.astype(jnp.float32))
    whole = jnp.concatenate(whole, axis=0).astype(jnp.bfloat16)
    for side in range(copies.shape[0]):
        copies[side] = whole


def project(attended, out_weight, residual, dev_count, side_count):
    batch_count, row_count, width = residual.shape
    rows = batch_count * row_count
    return pl.pallas_call(
        functools.partial(project_kernel, dev_count),
        out_shape=(
            jax.ShapeDtypeStruct((batch_count, row_count, width), jnp.bfloat16),
            jax.ShapeDtypeStruct((side_count, rows, width), jnp.bfloat16),
        ),
        in_specs=[vmem_spec] * (len(attended) + 2),
        out_specs=(vmem_spec, vmem_spec),
        compiler_params=pltpu.CompilerParams(vmem_limit_bytes=2 * mebibyte),
        cost_estimate=pl.CostEstimate(
            flops=hint_flops, transcendentals=0, bytes_accessed=out_weight.size * 2
        ),
        name="project",
    )(*attended, in_vmem(out_weight), residual)


def pieces_of(length, piece):
    return [(start, min(piece, length - start)) for start in range(0, length, piece)]


def normalize(parts, gain):
    width = sum(part.shape[1] for part in parts)
    center = sum(jnp.sum(part, axis=-1, keepdims=True) for part in parts) / width
    parts = [part - center for part in parts]
    spread = sum(jnp.sum(jnp.square(part), axis=-1, keepdims=True) for part in parts) / width
    values = jnp.concatenate(parts, axis=1) if len(parts) > 1 else parts[0]
    return values * lax.rsqrt(spread + norm_epsilon) * gain


def hidden_rows(parts, gain, w_gate, w_up, hidden):
    rows = normalize(parts, gain[...]).astype(jnp.bfloat16)
    for start, size in pieces_of(w_gate.shape[0], 896):
        span = slice(start, start + size)
        gate = lax.dot_general(w_gate[span, :], rows, last_last, preferred_element_type=jnp.float32)
        up = lax.dot_general(w_up[span, :], rows, last_last, preferred_element_type=jnp.float32)
        hidden[:, span] = (gate / (1.0 + jnp.exp(-gate)) * up).T.astype(jnp.bfloat16)


def mixed_plan(units, inner):
    own = units // mxu_count
    blocks = own // mxu_size
    rest = own - blocks * mxu_size
    return own, blocks, rest, (own + rest) // 2, inner // mxu_size


def mixed_products(normed, turned, w_gate, w_up, hidden, held, *sums):
    units, inner = w_gate.shape
    row_count = normed.shape[0]
    own, blocks, rest, streamed, depth = mixed_plan(units, inner)
    wide, narrow = sums[:mxu_count], sums[mxu_count:]

    def piece(index):
        return slice(index * mxu_size, (index + 1) * mxu_size)

    for turn in range(2):
        loaded = [(block, k) for block in range(blocks) for k in range(depth)]
        middle = (len(loaded) + 1) // 2
        loaded = loaded[:middle] if turn == 0 else loaded[middle:]
        steps, done = [], 0
        for k in range(depth):
            upto = (k + 1) * len(loaded) // depth
            steps += loaded[done : done + 1] + [(None, k)] + loaded[done + 1 : upto]
            done = upto

        def load(index, unit):
            block, k = steps[index]
            if block is None:
                pltpu.matmul_push_rhs(turned[piece(k), :], index % 2, unit)
            else:
                start = unit * own + block * mxu_size
                tile = w_up[start : start + mxu_size, piece(k)]
                pltpu.matmul_push_rhs(tile, index % 2, unit, transpose=True)

        def multiply(index, unit):
            block, k = steps[index]
            start, stop = unit * own, (unit + 1) * own
            if block is not None:
                target, left = narrow[unit * blocks + block], normed[:, piece(k)]
            elif turn == 0:
                target, left = wide[unit], w_gate[start : start + streamed, piece(k)]
            else:
                target, left = wide[unit], w_gate[start + streamed : stop, piece(k)]
                if rest:
                    left = jnp.concatenate([left, w_up[stop - rest : stop, piece(k)]], axis=0)
            pltpu.matmul_acc_lhs(target, left, load_staged_rhs=index % 2)

        for unit in range(mxu_count):
            load(0, unit)
            load(1, unit)
        for index in range(len(steps)):
            for unit in range(mxu_count):
                multiply(index, unit)
                if index + 2 < len(steps):
                    load(index + 2, unit)
        for unit in range(mxu_count):
            result = pltpu.matmul_pop(wide[unit])[:, :128]
            start = unit * own
            if turn == 0:
                held[start : start + streamed, :] = result
            else:
                held[start + streamed : start + own, :] = result[: own - streamed]
                if rest:
                    held[units + unit * rest : units + (unit + 1) * rest, :] = result[
                        own - streamed :
                    ]

    for unit in range(mxu_count):
        for block in range(blocks):
            start = unit * own + block * mxu_size
            up = pltpu.matmul_pop(narrow[unit * blocks + block])
            gate = held[start : start + mxu_size, :].T[:row_count]
            hidden[:, start : start + mxu_size] = (gate / (1.0 + jnp.exp(-gate)) * up).astype(
                jnp.bfloat16
            )
        if rest:
            start = unit * own + blocks * mxu_size
            gate = held[start : start + rest, :]
            up = held[units + unit * rest : units + (unit + 1) * rest, :]
            value = (gate / (1.0 + jnp.exp(-gate)) * up).T[:row_count]
            hidden[:, start : start + rest] = value.astype(jnp.bfloat16)


def loaded_products(hidden, weight, out, *sums):
    row_count, inner = hidden.shape
    blocks = out.shape[1] // mxu_size // mxu_count
    starts = list(range(0, inner - mxu_size + 1, mxu_size))
    left = inner - starts[-1] - mxu_size
    lefts = [hidden[:, start : start + mxu_size] for start in starts]
    if left:
        starts.append(inner - mxu_size)
        zeros = jnp.zeros((row_count, mxu_size - left), jnp.bfloat16)
        lefts.append(jnp.concatenate([zeros, hidden[:, inner - left :]], axis=1))
    steps = [(block, k) for block in range(blocks) for k in range(len(starts))]

    def load(index, unit):
        block, k = steps[index]
        column = (unit * blocks + block) * mxu_size
        tile = weight[starts[k] : starts[k] + mxu_size, column : column + mxu_size]
        pltpu.matmul_push_rhs(tile, index % 2, unit)

    for unit in range(mxu_count):
        load(0, unit)
        load(1, unit)
    for index, (block, k) in enumerate(steps):
        for unit in range(mxu_count):
            pltpu.matmul_acc_lhs(
                sums[unit * blocks + block], lefts[k], load_staged_rhs=index % 2
            )
            if index + 2 < len(steps):
                load(index + 2, unit)
        if k == len(starts) - 1:
            for unit in range(mxu_count):
                column = (unit * blocks + block) * mxu_size
                result = pltpu.matmul_pop(sums[unit * blocks + block])
                out[:, column : column + mxu_size] = result.astype(jnp.bfloat16)


def pair_kernel(own, other, gain, w_gate, w_up, w_down, hidden, given, kept, *scratch):
    lent, normed, turned, held, arrived = scratch
    dev_index = lax.axis_index("dev")
    row_count, width = own.shape
    units, inner = w_gate.shape
    copies = [
        pltpu.make_async_copy(
            w_down.at[:, pl.ds(pl.multiple_of(dev * width, width), width)],
            target,
            arrived.at[index],
        )
        for index, (dev, target) in enumerate(((1 - dev_index, lent), (dev_index, kept)))
    ]
    for copy in copies:
        copy.start()

    @pl.when(dev_index < 2)
    def _():
        parts = halves(dev_index, own[...].astype(jnp.float32), other[...].astype(jnp.float32))
        rows = normalize(parts, gain[...])
        normed[...] = rows.astype(jnp.bfloat16)
        columns = rows.T.astype(jnp.bfloat16)
        turned[:, :128] = jnp.concatenate(
            [columns, jnp.zeros((inner, 128 - row_count), jnp.bfloat16)], axis=1
        )
        turned[:, 128:] = jnp.zeros((inner, mxu_size - 128), jnp.bfloat16)
        _, blocks, _, streamed, _ = mixed_plan(units, inner)
        sums = [pltpu.ACC(unit)((streamed, mxu_size), jnp.float32) for unit in range(mxu_count)]
        for unit in range(mxu_count):
            sums += [pltpu.ACC(unit)((row_count, mxu_size), jnp.float32)] * blocks
        pl.run_scoped(
            functools.partial(mixed_products, normed, turned, w_gate, w_up, hidden, held), *sums
        )

    for copy in copies:
        copy.wait()
    blocks = width // mxu_size // mxu_count
    sums = [
        pltpu.ACC(unit)((row_count, mxu_size), jnp.float32)
        for unit in range(mxu_count)
        for _ in range(blocks)
    ]
    pl.run_scoped(functools.partial(loaded_products, hidden, lent, given), *sums)


def down_kernel(hidden, kept, out):
    out[...] = jnp.dot(hidden[...], kept[...], preferred_element_type=jnp.float32).astype(
        jnp.bfloat16
    )


def pair_experts(arrived, gain, w_gate, w_up, w_down):
    swap = [(0, 1), (1, 0)]
    rows, half = arrived.shape
    units, width = w_gate.shape
    hidden, given, kept = pl.pallas_call(
        pair_kernel,
        out_shape=(
            jax.ShapeDtypeStruct((rows, units), jnp.bfloat16),
            jax.ShapeDtypeStruct((rows, half), jnp.bfloat16),
            pltpu.VMEM((units, half), jnp.bfloat16),
        ),
        in_specs=[vmem_spec] * 5 + [pl.BlockSpec(memory_space=pl.ANY)],
        out_specs=(vmem_spec,) * 3,
        scratch_shapes=[
            pltpu.VMEM((units, half), jnp.bfloat16),
            pltpu.VMEM((rows, width), jnp.bfloat16),
            pltpu.VMEM((width, mxu_size), jnp.bfloat16),
            pltpu.VMEM((units + mxu_count * mxu_size, 128), jnp.float32),
            pltpu.SemaphoreType.DMA((2,)),
        ],
        compiler_params=pltpu.CompilerParams(vmem_limit_bytes=12 * mebibyte),
        name="experts",
    )(
        arrived,
        lax.ppermute(arrived, "dev", swap),
        gain.reshape(1, width),
        in_vmem(w_gate),
        in_vmem(w_up),
        in_hbm(w_down),
    )
    taken = lax.ppermute(given, "dev", swap)
    own = pl.pallas_call(
        down_kernel,
        out_shape=jax.ShapeDtypeStruct((rows, half), jnp.bfloat16),
        in_specs=[vmem_spec, vmem_spec],
        out_specs=vmem_spec,
        compiler_params=pltpu.CompilerParams(vmem_limit_bytes=2 * mebibyte),
        name="down_own",
    )(hidden, in_vmem(kept))
    return own.astype(jnp.float32) + taken.astype(jnp.float32)


def whole_kernel(rows, gain, w_gate, w_up, w_down, out, hidden):
    hidden_rows([rows[...].astype(jnp.float32)], gain, w_gate, w_up, hidden)
    out[...] = jnp.dot(hidden[...], w_down[...], preferred_element_type=jnp.float32).astype(
        jnp.bfloat16
    )


def whole_experts(arrived, gain, w_gate, w_up, w_down):
    rows, part_width = arrived.shape
    units, width = w_gate.shape
    block = min(rows, 128)
    gathered = lax.all_gather(arrived, "dev", axis=1, tiled=True)
    given = pl.pallas_call(
        whole_kernel,
        grid=(rows // block,),
        out_shape=jax.ShapeDtypeStruct((rows, width), jnp.bfloat16),
        in_specs=[pl.BlockSpec((block, width), lambda r: (r, 0))]
        + [pl.BlockSpec((1, width), lambda r: (0, 0)), vmem_spec, vmem_spec, vmem_spec],
        out_specs=pl.BlockSpec((block, width), lambda r: (r, 0)),
        scratch_shapes=[pltpu.VMEM((block, units), jnp.bfloat16)],
        compiler_params=pltpu.CompilerParams(vmem_limit_bytes=24 * mebibyte),
        name="experts",
    )(gathered, gain.reshape(1, width), w_gate, w_up, w_down)
    pieces = given.reshape(rows, width // part_width, part_width)
    pieces = lax.all_to_all(pieces, "dev", split_axis=1, concat_axis=1, tiled=True)
    return jnp.sum(pieces.astype(jnp.float32), axis=1)


def combine_kernel(shares, updated, returned, out):
    batch_count = updated.shape[0]
    for batch in range(batch_count):
        total = updated[batch].astype(jnp.float32)
        for expert in range(returned.shape[0]):
            share = shares[batch, :, expert : expert + 1]
            total = total + share * returned[expert, batch].astype(jnp.float32)
        out[batch] = total.astype(jnp.bfloat16)


def combine(shares, updated, returned):
    return pl.pallas_call(
        combine_kernel,
        out_shape=jax.ShapeDtypeStruct(updated.shape, jnp.bfloat16),
        in_specs=[vmem_spec] * 3,
        out_specs=vmem_spec,
        compiler_params=pltpu.CompilerParams(vmem_limit_bytes=8 * mebibyte),
        name="combine",
    )(shares, updated, returned)


def body(
    queries,
    cache_keys,
    cache_values,
    new_keys,
    new_values,
    lengths,
    out_weight,
    residual,
    norm_gain,
    routes,
    route_probs,
    w_gate,
    w_up,
    w_down,
):
    side_count = lax.axis_size("side")
    dev_count = lax.axis_size("dev")
    batch_count, row_count, _, column_width = residual.shape
    rows = batch_count * row_count
    swap = [(0, 1), (1, 0)]

    attended, shares = attend(
        queries, cache_keys, cache_values, new_keys, new_values, lengths, routes, route_probs
    )
    if dev_count == 2:
        attended = (attended, lax.ppermute(attended, "dev", swap))
    else:
        attended = (lax.all_gather(attended, "dev", axis=0, tiled=True),)
    updated, copies = project(
        attended,
        out_weight,
        residual.reshape(batch_count, row_count, column_width),
        dev_count,
        side_count,
    )
    arrived = lax.all_to_all(copies, "side", split_axis=0, concat_axis=0, tiled=True)
    arrived = arrived.reshape(side_count * rows, column_width)
    gather_and_run = pair_experts if dev_count == 2 else whole_experts
    total = gather_and_run(arrived, norm_gain, w_gate[0], w_up[0], w_down[0])
    total = total.astype(jnp.bfloat16).reshape(side_count, batch_count, row_count, column_width)
    returned = lax.all_to_all(total, "side", split_axis=0, concat_axis=0, tiled=True)
    result = combine(shares, updated, returned)
    return result.reshape(residual.shape)


def solution(mesh):
    placed = (
        P("groups", "dev", "side", None, None),
        P("groups", "dev", "side", None, None, None),
        P("groups", "dev", "side", None, None, None),
        P("groups", "dev", "side", None, None),
        P("groups", "dev", "side", None, None),
        P("groups", "dev", "side"),
        P(None, "dev"),
        P("groups", None, "side", "dev"),
        P(),
        P("groups", None, None, None),
        P("groups", None, "side", None),
        P("side", "dev", None),
        P("side", "dev", None),
        P("side", "dev", None),
    )
    return jax.shard_map(
        body,
        mesh=mesh,
        in_specs=placed,
        out_specs=P("groups", None, "side", "dev"),
        check_vma=False,
    )
```

```python
import functools
import math

import jax
import jax.numpy as jnp
from jax import lax
from jax.experimental import pallas as pl
from jax.experimental.pallas import tpu as pltpu
from jax.sharding import PartitionSpec as P

norm_epsilon = 1e-05
mebibyte = 1024 * 1024
mxu_count, mxu_size = 2, 256
hint_flops = 20_000_000_000
last_last = (((1,), (1,)), ((), ()))

smem_spec = pl.BlockSpec(memory_space=pltpu.SMEM)
vmem_spec = pl.BlockSpec(memory_space=pltpu.VMEM)
in_hbm = functools.partial(pltpu.with_memory_space_constraint, memory_space=pltpu.HBM)
in_vmem = functools.partial(pltpu.with_memory_space_constraint, memory_space=pltpu.VMEM)


def share_rows(routes, probs, shares):
    batch_count, row_count, _ = shares.shape
    top_count = routes.shape[2]
    side_index = lax.axis_index("side")
    row_ids = lax.broadcasted_iota(jnp.int32, shares.shape[1:], 0)
    lane_ids = lax.broadcasted_iota(jnp.int32, shares.shape[1:], 1)
    for batch in range(batch_count):

        def place(row, placed):
            for top in range(top_count):
                expert = routes[batch, row, top, side_index]
                placed = jnp.where(
                    (row_ids == row) & (lane_ids == expert), probs[batch, row, 0, top], placed
                )
            return placed

        placed = jnp.zeros(shares.shape[1:], jnp.float32)
        if row_count <= 8:
            for row in range(row_count):
                placed = place(row, placed)
        else:
            placed = lax.fori_loop(0, row_count, place, placed)
        shares[batch] = placed / jnp.sum(placed, axis=-1, keepdims=True)


def attend_kernel(
    lengths, routes, probs, queries, keys, values, new_keys, new_values, out, shares, scratch
):
    row_count, head_count, head_width = queries.shape
    pair_count = keys.shape[1]
    key_heads = new_keys.shape[1]
    width = head_count // key_heads
    local_rows = lengths.shape[2]
    factor = 1.0 / math.sqrt(head_width)
    pair = lax.broadcasted_iota(jnp.int32, (head_count, pair_count), 1)
    head = lax.broadcasted_iota(jnp.int32, (head_count, pair_count), 0)
    own_key = (pair % key_heads) == (head // width)
    position = jnp.where(own_key, pair // key_heads, pair_count)
    key_head = lax.broadcasted_iota(jnp.int32, (head_count, head_width), 0) // width

    def spread(block):
        wide = block.astype(jnp.float32)
        result = jnp.zeros((head_count, head_width), jnp.float32)
        for index in range(key_heads):
            result = jnp.where(key_head == index, wide[index : index + 1, :], result)
        return result

    all_rows = range(row_count)
    scores = [
        lax.dot_general(queries[row], keys[row], last_last, preferred_element_type=jnp.float32)
        for row in all_rows
    ]
    fresh = [
        jnp.sum(queries[row].astype(jnp.float32) * spread(new_keys[row]), axis=-1, keepdims=True)
        for row in all_rows
    ]
    lengths_of = [lengths[row // local_rows, 0, row % local_rows] for row in all_rows]
    raised = [
        jnp.where(position < lengths_of[row], jnp.exp(scores[row] * factor), 0.0)
        for row in all_rows
    ]
    raised_new = [jnp.exp(fresh[row] * factor) for row in all_rows]
    inverse = [
        1.0 / (jnp.sum(raised[row], axis=-1, keepdims=True) + raised_new[row]) for row in all_rows
    ]
    mixed = [
        jnp.dot(
            (raised[row] * inverse[row]).astype(jnp.bfloat16),
            values[row],
            preferred_element_type=jnp.float32,
        )
        for row in all_rows
    ]
    for row in all_rows:
        weight_new = (raised_new[row] * inverse[row]).astype(jnp.bfloat16).astype(jnp.float32)
        scratch[pl.ds(row * head_count, head_count), :] = mixed[row] + weight_new * spread(
            new_values[row]
        )
    pieces = [
        scratch[pl.ds(index, row_count, stride=head_count), :] for index in range(head_count)
    ]
    out[...] = jnp.concatenate(pieces, axis=1).astype(jnp.bfloat16)
    share_rows(routes, probs, shares)


def attend(queries, cache_keys, cache_values, new_keys, new_values, lengths, routes, probs):
    batch_count, local_rows = queries.shape[:2]
    rows = batch_count * local_rows
    head_count, head_width = queries.shape[-2:]
    key_heads = cache_keys.shape[-2]
    pairs = cache_keys.shape[-3] * key_heads
    return pl.pallas_call(
        attend_kernel,
        out_shape=(
            jax.ShapeDtypeStruct((rows, head_count * head_width), jnp.bfloat16),
            jax.ShapeDtypeStruct((batch_count, routes.shape[1], 128), jnp.float32),
        ),
        in_specs=[smem_spec] * 3 + [vmem_spec] * 5,
        out_specs=(vmem_spec, vmem_spec),
        scratch_shapes=[pltpu.VMEM((rows * head_count, head_width), jnp.float32)],
        compiler_params=pltpu.CompilerParams(vmem_limit_bytes=50 * mebibyte),
        name="attend",
        cost_estimate=pl.CostEstimate(
            flops=hint_flops, transcendentals=0, bytes_accessed=cache_keys.size * 4
        ),
    )(
        in_hbm(jnp.swapaxes(lengths, 1, 2)),
        in_hbm(jnp.swapaxes(routes, 2, 3)),
        in_hbm(probs),
        in_hbm(queries.reshape(rows, head_count, head_width)),
        in_hbm(cache_keys.reshape(rows, pairs, head_width)),
        in_hbm(cache_values.reshape(rows, pairs, head_width)),
        in_hbm(new_keys.reshape(rows, key_heads, head_width)),
        in_hbm(new_values.reshape(rows, key_heads, head_width)),
    )


def halves(dev_index, own, other):
    first = jnp.where(dev_index == 0, own, other)
    second = jnp.where(dev_index == 0, other, own)
    return first, second


def project_kernel(dev_count, *refs):
    attended, (out_weight, residual, updated, copies) = refs[:-4], refs[-4:]
    batch_count, row_count, _ = residual.shape
    local_rows = row_count // dev_count
    parts = [ref[...] for ref in attended]
    if len(parts) == 2:
        parts = [part.astype(jnp.float32) for part in parts]
        rows = jnp.concatenate(halves(lax.axis_index("dev"), *parts), axis=0).astype(jnp.bfloat16)
    else:
        rows = parts[0]
    result = jnp.dot(rows, out_weight[...], preferred_element_type=jnp.float32)
    whole = []
    for batch in range(batch_count):
        pieces = []
        for dev in range(dev_count):
            start = (dev * batch_count + batch) * local_rows
            pieces.append(result[start : start + local_rows, :])
        projected = jnp.concatenate(pieces, axis=0).astype(jnp.bfloat16)
        rows = (residual[batch].astype(jnp.float32) + projected.astype(jnp.float32)).astype(
            jnp.bfloat16
        )
        updated[batch] = rows
        whole.append(rows.astype(jnp.float32))
    whole = jnp.concatenate(whole, axis=0).astype(jnp.bfloat16)
    for side in range(copies.shape[0]):
        copies[side] = whole


def project(attended, out_weight, residual, dev_count, side_count):
    batch_count, row_count, width = residual.shape
    rows = batch_count * row_count
    return pl.pallas_call(
        functools.partial(project_kernel, dev_count),
        out_shape=(
            jax.ShapeDtypeStruct((batch_count, row_count, width), jnp.bfloat16),
            jax.ShapeDtypeStruct((side_count, rows, width), jnp.bfloat16),
        ),
        in_specs=[vmem_spec] * (len(attended) + 2),
        out_specs=(vmem_spec, vmem_spec),
        compiler_params=pltpu.CompilerParams(vmem_limit_bytes=2 * mebibyte),
        cost_estimate=pl.CostEstimate(
            flops=hint_flops, transcendentals=0, bytes_accessed=out_weight.size * 2
        ),
        name="project",
    )(*attended, in_vmem(out_weight), residual)


def pieces_of(length, piece):
    return [(start, min(piece, length - start)) for start in range(0, length, piece)]


def normalize(parts, gain):
    width = sum(part.shape[1] for part in parts)
    center = sum(jnp.sum(part, axis=-1, keepdims=True) for part in parts) / width
    parts = [part - center for part in parts]
    spread = sum(jnp.sum(jnp.square(part), axis=-1, keepdims=True) for part in parts) / width
    values = jnp.concatenate(parts, axis=1) if len(parts) > 1 else parts[0]
    return values * lax.rsqrt(spread + norm_epsilon) * gain


def hidden_rows(parts, gain, w_gate, w_up, hidden):
    rows = normalize(parts, gain[...]).astype(jnp.bfloat16)
    for start, size in pieces_of(w_gate.shape[0], 896):
        span = slice(start, start + size)
        gate = lax.dot_general(w_gate[span, :], rows, last_last, preferred_element_type=jnp.float32)
        up = lax.dot_general(w_up[span, :], rows, last_last, preferred_element_type=jnp.float32)
        hidden[:, span] = (gate / (1.0 + jnp.exp(-gate)) * up).T.astype(jnp.bfloat16)


def mixed_plan(units, inner):
    own = units // mxu_count
    blocks = own // mxu_size
    rest = own - blocks * mxu_size
    return own, blocks, rest, (own + rest) // 2, inner // mxu_size


def mixed_products(normed, turned, w_gate, w_up, hidden, held, *sums):
    units, inner = w_gate.shape
    row_count = normed.shape[0]
    own, blocks, rest, streamed, depth = mixed_plan(units, inner)
    wide, narrow = sums[:mxu_count], sums[mxu_count:]

    def piece(index):
        return slice(index * mxu_size, (index + 1) * mxu_size)

    for turn in range(2):
        loaded = [(block, k) for block in range(blocks) for k in range(depth)]
        middle = (len(loaded) + 1) // 2
        loaded = loaded[:middle] if turn == 0 else loaded[middle:]
        steps, done = [], 0
        for k in range(depth):
            upto = (k + 1) * len(loaded) // depth
            steps += loaded[done : done + 1] + [(None, k)] + loaded[done + 1 : upto]
            done = upto

        def load(index, unit):
            block, k = steps[index]
            if block is None:
                pltpu.matmul_push_rhs(turned[piece(k), :], index % 2, unit)
            else:
                start = unit * own + block * mxu_size
                tile = w_up[start : start + mxu_size, piece(k)]
                pltpu.matmul_push_rhs(tile, index % 2, unit, transpose=True)

        def multiply(index, unit):
            block, k = steps[index]
            start, stop = unit * own, (unit + 1) * own
            if block is not None:
                target, left = narrow[unit * blocks + block], normed[:, piece(k)]
            elif turn == 0:
                target, left = wide[unit], w_gate[start : start + streamed, piece(k)]
            else:
                target, left = wide[unit], w_gate[start + streamed : stop, piece(k)]
                if rest:
                    left = jnp.concatenate([left, w_up[stop - rest : stop, piece(k)]], axis=0)
            pltpu.matmul_acc_lhs(target, left, load_staged_rhs=index % 2)

        for unit in range(mxu_count):
            load(0, unit)
            load(1, unit)
        for index in range(len(steps)):
            for unit in range(mxu_count):
                multiply(index, unit)
                if index + 2 < len(steps):
                    load(index + 2, unit)
        for unit in range(mxu_count):
            result = pltpu.matmul_pop(wide[unit])[:, :128]
            start = unit * own
            if turn == 0:
                held[start : start + streamed, :] = result
            else:
                held[start + streamed : start + own, :] = result[: own - streamed]
                if rest:
                    held[units + unit * rest : units + (unit + 1) * rest, :] = result[
                        own - streamed :
                    ]

    for unit in range(mxu_count):
        for block in range(blocks):
            start = unit * own + block * mxu_size
            up = pltpu.matmul_pop(narrow[unit * blocks + block])
            gate = held[start : start + mxu_size, :].T[:row_count]
            hidden[:, start : start + mxu_size] = (gate / (1.0 + jnp.exp(-gate)) * up).astype(
                jnp.bfloat16
            )
        if rest:
            start = unit * own + blocks * mxu_size
            gate = held[start : start + rest, :]
            up = held[units + unit * rest : units + (unit + 1) * rest, :]
            value = (gate / (1.0 + jnp.exp(-gate)) * up).T[:row_count]
            hidden[:, start : start + rest] = value.astype(jnp.bfloat16)


def loaded_products(hidden, weight, out, *sums):
    row_count, inner = hidden.shape
    blocks = out.shape[1] // mxu_size // mxu_count
    starts = list(range(0, inner - mxu_size + 1, mxu_size))
    left = inner - starts[-1] - mxu_size
    lefts = [hidden[:, start : start + mxu_size] for start in starts]
    if left:
        starts.append(inner - mxu_size)
        zeros = jnp.zeros((row_count, mxu_size - left), jnp.bfloat16)
        lefts.append(jnp.concatenate([zeros, hidden[:, inner - left :]], axis=1))
    steps = [(block, k) for block in range(blocks) for k in range(len(starts))]

    def load(index, unit):
        block, k = steps[index]
        column = (unit * blocks + block) * mxu_size
        tile = weight[starts[k] : starts[k] + mxu_size, column : column + mxu_size]
        pltpu.matmul_push_rhs(tile, index % 2, unit)

    for unit in range(mxu_count):
        load(0, unit)
        load(1, unit)
    for index, (block, k) in enumerate(steps):
        for unit in range(mxu_count):
            pltpu.matmul_acc_lhs(
                sums[unit * blocks + block], lefts[k], load_staged_rhs=index % 2
            )
            if index + 2 < len(steps):
                load(index + 2, unit)
        if k == len(starts) - 1:
            for unit in range(mxu_count):
                column = (unit * blocks + block) * mxu_size
                result = pltpu.matmul_pop(sums[unit * blocks + block])
                out[:, column : column + mxu_size] = result.astype(jnp.bfloat16)


def pair_kernel(own, other, gain, w_gate, w_up, w_down, hidden, given, kept, *scratch):
    lent, normed, turned, held, arrived = scratch
    dev_index = lax.axis_index("dev")
    row_count, width = own.shape
    units, inner = w_gate.shape
    copies = [
        pltpu.make_async_copy(
            w_down.at[:, pl.ds(pl.multiple_of(dev * width, width), width)],
            target,
            arrived.at[index],
        )
        for index, (dev, target) in enumerate(((1 - dev_index, lent), (dev_index, kept)))
    ]
    for copy in copies:
        copy.start()

    @pl.when(dev_index < 2)
    def _():
        parts = halves(dev_index, own[...].astype(jnp.float32), other[...].astype(jnp.float32))
        rows = normalize(parts, gain[...])
        normed[...] = rows.astype(jnp.bfloat16)
        columns = rows.T.astype(jnp.bfloat16)
        turned[:, :128] = jnp.concatenate(
            [columns, jnp.zeros((inner, 128 - row_count), jnp.bfloat16)], axis=1
        )
        turned[:, 128:] = jnp.zeros((inner, mxu_size - 128), jnp.bfloat16)
        _, blocks, _, streamed, _ = mixed_plan(units, inner)
        sums = [pltpu.ACC(unit)((streamed, mxu_size), jnp.float32) for unit in range(mxu_count)]
        for unit in range(mxu_count):
            sums += [pltpu.ACC(unit)((row_count, mxu_size), jnp.float32)] * blocks
        pl.run_scoped(
            functools.partial(mixed_products, normed, turned, w_gate, w_up, hidden, held), *sums
        )

    for copy in copies:
        copy.wait()
    blocks = width // mxu_size // mxu_count
    sums = [
        pltpu.ACC(unit)((row_count, mxu_size), jnp.float32)
        for unit in range(mxu_count)
        for _ in range(blocks)
    ]
    pl.run_scoped(functools.partial(loaded_products, hidden, lent, given), *sums)


def down_kernel(hidden, kept, out):
    out[...] = jnp.dot(hidden[...], kept[...], preferred_element_type=jnp.float32).astype(
        jnp.bfloat16
    )


def pair_experts(arrived, gain, w_gate, w_up, w_down):
    swap = [(0, 1), (1, 0)]
    rows, half = arrived.shape
    units, width = w_gate.shape
    hidden, given, kept = pl.pallas_call(
        pair_kernel,
        out_shape=(
            jax.ShapeDtypeStruct((rows, units), jnp.bfloat16),
            jax.ShapeDtypeStruct((rows, half), jnp.bfloat16),
            pltpu.VMEM((units, half), jnp.bfloat16),
        ),
        in_specs=[vmem_spec] * 5 + [pl.BlockSpec(memory_space=pl.ANY)],
        out_specs=(vmem_spec,) * 3,
        scratch_shapes=[
            pltpu.VMEM((units, half), jnp.bfloat16),
            pltpu.VMEM((rows, width), jnp.bfloat16),
            pltpu.VMEM((width, mxu_size), jnp.bfloat16),
            pltpu.VMEM((units + mxu_count * mxu_size, 128), jnp.float32),
            pltpu.SemaphoreType.DMA((2,)),
        ],
        compiler_params=pltpu.CompilerParams(vmem_limit_bytes=12 * mebibyte),
        name="experts",
    )(
        arrived,
        lax.ppermute(arrived, "dev", swap),
        gain.reshape(1, width),
        in_vmem(w_gate),
        in_vmem(w_up),
        in_hbm(w_down),
    )
    taken = lax.ppermute(given, "dev", swap)
    own = pl.pallas_call(
        down_kernel,
        out_shape=jax.ShapeDtypeStruct((rows, half), jnp.bfloat16),
        in_specs=[vmem_spec, vmem_spec],
        out_specs=vmem_spec,
        compiler_params=pltpu.CompilerParams(vmem_limit_bytes=2 * mebibyte),
        name="down_own",
    )(hidden, in_vmem(kept))
    return own.astype(jnp.float32) + taken.astype(jnp.float32)


def whole_kernel(rows, gain, w_gate, w_up, w_down, out, hidden):
    hidden_rows([rows[...].astype(jnp.float32)], gain, w_gate, w_up, hidden)
    out[...] = jnp.dot(hidden[...], w_down[...], preferred_element_type=jnp.float32).astype(
        jnp.bfloat16
    )


def whole_experts(arrived, gain, w_gate, w_up, w_down):
    rows, part_width = arrived.shape
    units, width = w_gate.shape
    block = min(rows, 128)
    gathered = lax.all_gather(arrived, "dev", axis=1, tiled=True)
    given = pl.pallas_call(
        whole_kernel,
        grid=(rows // block,),
        out_shape=jax.ShapeDtypeStruct((rows, width), jnp.bfloat16),
        in_specs=[pl.BlockSpec((block, width), lambda r: (r, 0))]
        + [pl.BlockSpec((1, width), lambda r: (0, 0)), vmem_spec, vmem_spec, vmem_spec],
        out_specs=pl.BlockSpec((block, width), lambda r: (r, 0)),
        scratch_shapes=[pltpu.VMEM((block, units), jnp.bfloat16)],
        compiler_params=pltpu.CompilerParams(vmem_limit_bytes=24 * mebibyte),
        name="experts",
    )(gathered, gain.reshape(1, width), w_gate, w_up, w_down)
    pieces = given.reshape(rows, width // part_width, part_width)
    pieces = lax.all_to_all(pieces, "dev", split_axis=1, concat_axis=1, tiled=True)
    return jnp.sum(pieces.astype(jnp.float32), axis=1)


def combine_kernel(shares, updated, returned, out):
    batch_count, row_count, _ = updated.shape
    weights = jnp.concatenate([shares[batch] for batch in range(batch_count)], axis=0)
    total = jnp.concatenate(
        [updated[batch].astype(jnp.float32) for batch in range(batch_count)], axis=0
    )
    for expert in range(returned.shape[0]):
        total = total + weights[:, expert : expert + 1] * returned[expert].astype(jnp.float32)
    for batch in range(batch_count):
        out[batch] = total[batch * row_count : (batch + 1) * row_count].astype(jnp.bfloat16)


def combine(shares, updated, returned):
    return pl.pallas_call(
        combine_kernel,
        out_shape=jax.ShapeDtypeStruct(updated.shape, jnp.bfloat16),
        in_specs=[vmem_spec] * 3,
        out_specs=vmem_spec,
        compiler_params=pltpu.CompilerParams(vmem_limit_bytes=8 * mebibyte),
        name="combine",
    )(shares, updated, returned)


def body(
    queries,
    cache_keys,
    cache_values,
    new_keys,
    new_values,
    lengths,
    out_weight,
    residual,
    norm_gain,
    routes,
    route_probs,
    w_gate,
    w_up,
    w_down,
):
    side_count = lax.axis_size("side")
    dev_count = lax.axis_size("dev")
    batch_count, row_count, _, column_width = residual.shape
    rows = batch_count * row_count
    swap = [(0, 1), (1, 0)]

    attended, shares = attend(
        queries, cache_keys, cache_values, new_keys, new_values, lengths, routes, route_probs
    )
    if dev_count == 2:
        attended = (attended, lax.ppermute(attended, "dev", swap))
    else:
        attended = (lax.all_gather(attended, "dev", axis=0, tiled=True),)
    updated, copies = project(
        attended,
        out_weight,
        residual.reshape(batch_count, row_count, column_width),
        dev_count,
        side_count,
    )
    arrived = lax.all_to_all(copies, "side", split_axis=0, concat_axis=0, tiled=True)
    arrived = arrived.reshape(side_count * rows, column_width)
    gather_and_run = pair_experts if dev_count == 2 else whole_experts
    total = gather_and_run(arrived, norm_gain, w_gate[0], w_up[0], w_down[0])
    total = total.astype(jnp.bfloat16).reshape(side_count, rows, column_width)
    returned = lax.all_to_all(total, "side", split_axis=0, concat_axis=0, tiled=True)
    result = combine(shares, updated, returned)
    return result.reshape(residual.shape)


def solution(mesh):
    placed = (
        P("groups", "dev", "side", None, None),
        P("groups", "dev", "side", None, None, None),
        P("groups", "dev", "side", None, None, None),
        P("groups", "dev", "side", None, None),
        P("groups", "dev", "side", None, None),
        P("groups", "dev", "side"),
        P(None, "dev"),
        P("groups", None, "side", "dev"),
        P(),
        P("groups", None, None, None),
        P("groups", None, "side", None),
        P("side", "dev", None),
        P("side", "dev", None),
        P("side", "dev", None),
    )
    return jax.shard_map(
        body,
        mesh=mesh,
        in_specs=placed,
        out_specs=P("groups", None, "side", "dev"),
        check_vma=False,
    )
```

```python
import functools
import math

import jax
import jax.numpy as jnp
from jax import lax
from jax.experimental import pallas as pl
from jax.experimental.pallas import tpu as pltpu
from jax.sharding import PartitionSpec as P

norm_epsilon = 1e-05
mebibyte = 1024 * 1024
mxu_count, mxu_size = 2, 256
hint_flops = 20_000_000_000
last_last = (((1,), (1,)), ((), ()))

smem_spec = pl.BlockSpec(memory_space=pltpu.SMEM)
vmem_spec = pl.BlockSpec(memory_space=pltpu.VMEM)
in_hbm = functools.partial(pltpu.with_memory_space_constraint, memory_space=pltpu.HBM)
in_vmem = functools.partial(pltpu.with_memory_space_constraint, memory_space=pltpu.VMEM)


def share_rows(routes, probs, shares):
    batch_count, row_count, _ = shares.shape
    top_count = routes.shape[2]
    side_index = lax.axis_index("side")
    row_ids = lax.broadcasted_iota(jnp.int32, shares.shape[1:], 0)
    lane_ids = lax.broadcasted_iota(jnp.int32, shares.shape[1:], 1)
    for batch in range(batch_count):

        def place(row, placed):
            for top in range(top_count):
                expert = routes[batch, row, top, side_index]
                placed = jnp.where(
                    (row_ids == row) & (lane_ids == expert), probs[batch, row, 0, top], placed
                )
            return placed

        placed = jnp.zeros(shares.shape[1:], jnp.float32)
        if row_count <= 8:
            for row in range(row_count):
                placed = place(row, placed)
        else:
            placed = lax.fori_loop(0, row_count, place, placed)
        shares[batch] = placed / jnp.sum(placed, axis=-1, keepdims=True)


def attend_kernel(
    lengths, routes, probs, queries, keys, values, new_keys, new_values, out, shares, scratch
):
    row_count, head_count, head_width = queries.shape
    pair_count = keys.shape[1]
    key_heads = new_keys.shape[1]
    width = head_count // key_heads
    local_rows = lengths.shape[2]
    factor = 1.0 / math.sqrt(head_width)
    pair = lax.broadcasted_iota(jnp.int32, (head_count, pair_count), 1)
    head = lax.broadcasted_iota(jnp.int32, (head_count, pair_count), 0)
    own_key = (pair % key_heads) == (head // width)
    position = jnp.where(own_key, pair // key_heads, pair_count)
    key_head = lax.broadcasted_iota(jnp.int32, (head_count, head_width), 0) // width

    def spread(block):
        wide = block.astype(jnp.float32)
        result = jnp.zeros((head_count, head_width), jnp.float32)
        for index in range(key_heads):
            result = jnp.where(key_head == index, wide[index : index + 1, :], result)
        return result

    all_rows = range(row_count)
    scores = [
        lax.dot_general(queries[row], keys[row], last_last, preferred_element_type=jnp.float32)
        for row in all_rows
    ]
    fresh = [
        jnp.sum(queries[row].astype(jnp.float32) * spread(new_keys[row]), axis=-1, keepdims=True)
        for row in all_rows
    ]
    lengths_of = [lengths[row // local_rows, 0, row % local_rows] for row in all_rows]
    raised = [
        jnp.where(position < lengths_of[row], jnp.exp(scores[row] * factor), 0.0)
        for row in all_rows
    ]
    raised_new = [jnp.exp(fresh[row] * factor) for row in all_rows]
    inverse = [
        1.0 / (jnp.sum(raised[row], axis=-1, keepdims=True) + raised_new[row]) for row in all_rows
    ]
    mixed = [
        jnp.dot(
            (raised[row] * inverse[row]).astype(jnp.bfloat16),
            values[row],
            preferred_element_type=jnp.float32,
        )
        for row in all_rows
    ]
    for row in all_rows:
        weight_new = (raised_new[row] * inverse[row]).astype(jnp.bfloat16).astype(jnp.float32)
        scratch[pl.ds(row * head_count, head_count), :] = mixed[row] + weight_new * spread(
            new_values[row]
        )
    pieces = [
        scratch[pl.ds(index, row_count, stride=head_count), :] for index in range(head_count)
    ]
    out[...] = jnp.concatenate(pieces, axis=1).astype(jnp.bfloat16)
    share_rows(routes, probs, shares)


def attend(queries, cache_keys, cache_values, new_keys, new_values, lengths, routes, probs):
    batch_count, local_rows = queries.shape[:2]
    rows = batch_count * local_rows
    head_count, head_width = queries.shape[-2:]
    key_heads = cache_keys.shape[-2]
    pairs = cache_keys.shape[-3] * key_heads
    return pl.pallas_call(
        attend_kernel,
        out_shape=(
            jax.ShapeDtypeStruct((rows, head_count * head_width), jnp.bfloat16),
            jax.ShapeDtypeStruct((batch_count, routes.shape[1], 128), jnp.float32),
        ),
        in_specs=[smem_spec] * 3 + [vmem_spec] * 5,
        out_specs=(vmem_spec, vmem_spec),
        scratch_shapes=[pltpu.VMEM((rows * head_count, head_width), jnp.float32)],
        compiler_params=pltpu.CompilerParams(vmem_limit_bytes=50 * mebibyte),
        name="attend",
        cost_estimate=pl.CostEstimate(
            flops=hint_flops, transcendentals=0, bytes_accessed=cache_keys.size * 4
        ),
    )(
        in_hbm(jnp.swapaxes(lengths, 1, 2)),
        in_hbm(jnp.swapaxes(routes, 2, 3)),
        in_hbm(probs),
        in_hbm(queries.reshape(rows, head_count, head_width)),
        in_hbm(cache_keys.reshape(rows, pairs, head_width)),
        in_hbm(cache_values.reshape(rows, pairs, head_width)),
        in_hbm(new_keys.reshape(rows, key_heads, head_width)),
        in_hbm(new_values.reshape(rows, key_heads, head_width)),
    )


def halves(dev_index, own, other):
    first = jnp.where(dev_index == 0, own, other)
    second = jnp.where(dev_index == 0, other, own)
    return first, second


def project_kernel(dev_count, *refs):
    attended, (out_weight, residual, updated, copies) = refs[:-4], refs[-4:]
    batch_count, row_count, _ = residual.shape
    local_rows = row_count // dev_count
    parts = [ref[...] for ref in attended]
    if len(parts) == 2:
        parts = [part.astype(jnp.float32) for part in parts]
        rows = jnp.concatenate(halves(lax.axis_index("dev"), *parts), axis=0).astype(jnp.bfloat16)
    else:
        rows = parts[0]
    result = jnp.dot(rows, out_weight[...], preferred_element_type=jnp.float32)
    whole = []
    for batch in range(batch_count):
        pieces = []
        for dev in range(dev_count):
            start = (dev * batch_count + batch) * local_rows
            pieces.append(result[start : start + local_rows, :])
        projected = jnp.concatenate(pieces, axis=0).astype(jnp.bfloat16)
        rows = (residual[batch].astype(jnp.float32) + projected.astype(jnp.float32)).astype(
            jnp.bfloat16
        )
        updated[batch] = rows
        whole.append(rows.astype(jnp.float32))
    whole = jnp.concatenate(whole, axis=0).astype(jnp.bfloat16)
    for side in range(copies.shape[0]):
        copies[side] = whole


def project(attended, out_weight, residual, dev_count, side_count):
    batch_count, row_count, width = residual.shape
    rows = batch_count * row_count
    return pl.pallas_call(
        functools.partial(project_kernel, dev_count),
        out_shape=(
            jax.ShapeDtypeStruct((batch_count, row_count, width), jnp.bfloat16),
            jax.ShapeDtypeStruct((side_count, rows, width), jnp.bfloat16),
        ),
        in_specs=[vmem_spec] * (len(attended) + 2),
        out_specs=(vmem_spec, vmem_spec),
        compiler_params=pltpu.CompilerParams(vmem_limit_bytes=2 * mebibyte),
        cost_estimate=pl.CostEstimate(
            flops=hint_flops, transcendentals=0, bytes_accessed=out_weight.size * 2
        ),
        name="project",
    )(*attended, in_vmem(out_weight), residual)


def pieces_of(length, piece):
    return [(start, min(piece, length - start)) for start in range(0, length, piece)]


def normalize(parts, gain):
    width = sum(part.shape[1] for part in parts)
    center = sum(jnp.sum(part, axis=-1, keepdims=True) for part in parts) / width
    parts = [part - center for part in parts]
    spread = sum(jnp.sum(jnp.square(part), axis=-1, keepdims=True) for part in parts) / width
    values = jnp.concatenate(parts, axis=1) if len(parts) > 1 else parts[0]
    return values * lax.rsqrt(spread + norm_epsilon) * gain


def hidden_rows(parts, gain, w_gate, w_up, hidden):
    rows = normalize(parts, gain[...]).astype(jnp.bfloat16)
    for start, size in pieces_of(w_gate.shape[0], 896):
        span = slice(start, start + size)
        gate = lax.dot_general(w_gate[span, :], rows, last_last, preferred_element_type=jnp.float32)
        up = lax.dot_general(w_up[span, :], rows, last_last, preferred_element_type=jnp.float32)
        hidden[:, span] = (gate / (1.0 + jnp.exp(-gate)) * up).T.astype(jnp.bfloat16)


def mixed_plan(units, inner):
    own = units // mxu_count
    blocks = own // mxu_size
    rest = own - blocks * mxu_size
    return own, blocks, rest, (own + rest) // 2, inner // mxu_size


def mixed_products(normed, turned, w_gate, w_up, hidden, held, *sums):
    units, inner = w_gate.shape
    row_count = normed.shape[0]
    own, blocks, rest, streamed, depth = mixed_plan(units, inner)
    wide, narrow = sums[:mxu_count], sums[mxu_count:]

    def piece(index):
        return slice(index * mxu_size, (index + 1) * mxu_size)

    def finish(block):
        for unit in range(mxu_count):
            start = unit * own + block * mxu_size
            up = pltpu.matmul_pop(narrow[unit * blocks + block])
            gate = held[start : start + mxu_size, :].T[:row_count]
            hidden[:, start : start + mxu_size] = (gate / (1.0 + jnp.exp(-gate)) * up).astype(
                jnp.bfloat16
            )

    finished = 0
    for turn in range(2):
        loaded = [(block, k) for block in range(blocks) for k in range(depth)]
        middle = (len(loaded) + 1) // 2
        loaded = loaded[:middle] if turn == 0 else loaded[middle:]
        steps, done = [], 0
        for k in range(depth):
            upto = (k + 1) * len(loaded) // depth
            steps += loaded[done : done + 1] + [(None, k)] + loaded[done + 1 : upto]
            done = upto

        def load(index, unit):
            block, k = steps[index]
            if block is None:
                pltpu.matmul_push_rhs(turned[piece(k), :], index % 2, unit)
            else:
                start = unit * own + block * mxu_size
                tile = w_up[start : start + mxu_size, piece(k)]
                pltpu.matmul_push_rhs(tile, index % 2, unit, transpose=True)

        def multiply(index, unit):
            block, k = steps[index]
            start, stop = unit * own, (unit + 1) * own
            if block is not None:
                target, left = narrow[unit * blocks + block], normed[:, piece(k)]
            elif turn == 0:
                target, left = wide[unit], w_gate[start : start + streamed, piece(k)]
            else:
                target, left = wide[unit], w_gate[start + streamed : stop, piece(k)]
                if rest:
                    left = jnp.concatenate([left, w_up[stop - rest : stop, piece(k)]], axis=0)
            pltpu.matmul_acc_lhs(target, left, load_staged_rhs=index % 2)

        for unit in range(mxu_count):
            load(0, unit)
            load(1, unit)
        for index in range(len(steps)):
            for unit in range(mxu_count):
                multiply(index, unit)
                if index + 2 < len(steps):
                    load(index + 2, unit)
        for unit in range(mxu_count):
            result = pltpu.matmul_pop(wide[unit])[:, :128]
            start = unit * own
            if turn == 0:
                held[start : start + streamed, :] = result
            else:
                held[start + streamed : start + own, :] = result[: own - streamed]
                if rest:
                    held[units + unit * rest : units + (unit + 1) * rest, :] = result[
                        own - streamed :
                    ]

        ready = blocks if turn else min(middle // depth, streamed // mxu_size)
        for block in range(finished, ready):
            finish(block)
        finished = ready

    for unit in range(mxu_count):
        if rest:
            start = unit * own + blocks * mxu_size
            gate = held[start : start + rest, :]
            up = held[units + unit * rest : units + (unit + 1) * rest, :]
            value = (gate / (1.0 + jnp.exp(-gate)) * up).T[:row_count]
            hidden[:, start : start + rest] = value.astype(jnp.bfloat16)


def loaded_products(hidden, weight, out, *sums):
    row_count, inner = hidden.shape
    blocks = out.shape[1] // mxu_size // mxu_count
    starts = list(range(0, inner - mxu_size + 1, mxu_size))
    left = inner - starts[-1] - mxu_size
    lefts = [hidden[:, start : start + mxu_size] for start in starts]
    if left:
        starts.append(inner - mxu_size)
        zeros = jnp.zeros((row_count, mxu_size - left), jnp.bfloat16)
        lefts.append(jnp.concatenate([zeros, hidden[:, inner - left :]], axis=1))
    steps = [(block, k) for block in range(blocks) for k in range(len(starts))]

    def load(index, unit):
        block, k = steps[index]
        column = (unit * blocks + block) * mxu_size
        tile = weight[starts[k] : starts[k] + mxu_size, column : column + mxu_size]
        pltpu.matmul_push_rhs(tile, index % 2, unit)

    for unit in range(mxu_count):
        load(0, unit)
        load(1, unit)
    for index, (block, k) in enumerate(steps):
        for unit in range(mxu_count):
            pltpu.matmul_acc_lhs(
                sums[unit * blocks + block], lefts[k], load_staged_rhs=index % 2
            )
            if index + 2 < len(steps):
                load(index + 2, unit)
        if k == len(starts) - 1:
            for unit in range(mxu_count):
                column = (unit * blocks + block) * mxu_size
                result = pltpu.matmul_pop(sums[unit * blocks + block])
                out[:, column : column + mxu_size] = result.astype(jnp.bfloat16)


def pair_kernel(own, other, gain, w_gate, w_up, w_down, hidden, given, kept, *scratch):
    lent, normed, turned, held, arrived = scratch
    dev_index = lax.axis_index("dev")
    row_count, width = own.shape
    units, inner = w_gate.shape
    copies = [
        pltpu.make_async_copy(
            w_down.at[:, pl.ds(pl.multiple_of(dev * width, width), width)],
            target,
            arrived.at[index],
        )
        for index, (dev, target) in enumerate(((1 - dev_index, lent), (dev_index, kept)))
    ]
    for copy in copies:
        copy.start()

    @pl.when(dev_index < 2)
    def _():
        parts = halves(dev_index, own[...].astype(jnp.float32), other[...].astype(jnp.float32))
        rows = normalize(parts, gain[...])
        normed[...] = rows.astype(jnp.bfloat16)
        columns = rows.T.astype(jnp.bfloat16)
        turned[:, :128] = jnp.concatenate(
            [columns, jnp.zeros((inner, 128 - row_count), jnp.bfloat16)], axis=1
        )
        turned[:, 128:] = jnp.zeros((inner, mxu_size - 128), jnp.bfloat16)
        _, blocks, _, streamed, _ = mixed_plan(units, inner)
        sums = [pltpu.ACC(unit)((streamed, mxu_size), jnp.float32) for unit in range(mxu_count)]
        for unit in range(mxu_count):
            sums += [pltpu.ACC(unit)((row_count, mxu_size), jnp.float32)] * blocks
        pl.run_scoped(
            functools.partial(mixed_products, normed, turned, w_gate, w_up, hidden, held), *sums
        )

    for copy in copies:
        copy.wait()
    blocks = width // mxu_size // mxu_count
    sums = [
        pltpu.ACC(unit)((row_count, mxu_size), jnp.float32)
        for unit in range(mxu_count)
        for _ in range(blocks)
    ]
    pl.run_scoped(functools.partial(loaded_products, hidden, lent, given), *sums)


def down_kernel(hidden, kept, out):
    out[...] = jnp.dot(hidden[...], kept[...], preferred_element_type=jnp.float32).astype(
        jnp.bfloat16
    )


def pair_experts(arrived, gain, w_gate, w_up, w_down):
    swap = [(0, 1), (1, 0)]
    rows, half = arrived.shape
    units, width = w_gate.shape
    hidden, given, kept = pl.pallas_call(
        pair_kernel,
        out_shape=(
            jax.ShapeDtypeStruct((rows, units), jnp.bfloat16),
            jax.ShapeDtypeStruct((rows, half), jnp.bfloat16),
            pltpu.VMEM((units, half), jnp.bfloat16),
        ),
        in_specs=[vmem_spec] * 5 + [pl.BlockSpec(memory_space=pl.ANY)],
        out_specs=(vmem_spec,) * 3,
        scratch_shapes=[
            pltpu.VMEM((units, half), jnp.bfloat16),
            pltpu.VMEM((rows, width), jnp.bfloat16),
            pltpu.VMEM((width, mxu_size), jnp.bfloat16),
            pltpu.VMEM((units + mxu_count * mxu_size, 128), jnp.float32),
            pltpu.SemaphoreType.DMA((2,)),
        ],
        compiler_params=pltpu.CompilerParams(vmem_limit_bytes=12 * mebibyte),
        name="experts",
    )(
        arrived,
        lax.ppermute(arrived, "dev", swap),
        gain.reshape(1, width),
        in_vmem(w_gate),
        in_vmem(w_up),
        in_hbm(w_down),
    )
    taken = lax.ppermute(given, "dev", swap)
    own = pl.pallas_call(
        down_kernel,
        out_shape=jax.ShapeDtypeStruct((rows, half), jnp.bfloat16),
        in_specs=[vmem_spec, vmem_spec],
        out_specs=vmem_spec,
        compiler_params=pltpu.CompilerParams(vmem_limit_bytes=2 * mebibyte),
        name="down_own",
    )(hidden, in_vmem(kept))
    return own.astype(jnp.float32) + taken.astype(jnp.float32)


def whole_kernel(rows, gain, w_gate, w_up, w_down, out, hidden):
    hidden_rows([rows[...].astype(jnp.float32)], gain, w_gate, w_up, hidden)
    out[...] = jnp.dot(hidden[...], w_down[...], preferred_element_type=jnp.float32).astype(
        jnp.bfloat16
    )


def whole_experts(arrived, gain, w_gate, w_up, w_down):
    rows, part_width = arrived.shape
    units, width = w_gate.shape
    block = min(rows, 128)
    gathered = lax.all_gather(arrived, "dev", axis=1, tiled=True)
    given = pl.pallas_call(
        whole_kernel,
        grid=(rows // block,),
        out_shape=jax.ShapeDtypeStruct((rows, width), jnp.bfloat16),
        in_specs=[pl.BlockSpec((block, width), lambda r: (r, 0))]
        + [pl.BlockSpec((1, width), lambda r: (0, 0)), vmem_spec, vmem_spec, vmem_spec],
        out_specs=pl.BlockSpec((block, width), lambda r: (r, 0)),
        scratch_shapes=[pltpu.VMEM((block, units), jnp.bfloat16)],
        compiler_params=pltpu.CompilerParams(vmem_limit_bytes=24 * mebibyte),
        name="experts",
    )(gathered, gain.reshape(1, width), w_gate, w_up, w_down)
    pieces = given.reshape(rows, width // part_width, part_width)
    pieces = lax.all_to_all(pieces, "dev", split_axis=1, concat_axis=1, tiled=True)
    return jnp.sum(pieces.astype(jnp.float32), axis=1)


def combine_kernel(shares, updated, returned, out):
    batch_count, row_count, _ = updated.shape
    weights = jnp.concatenate([shares[batch] for batch in range(batch_count)], axis=0)
    total = jnp.concatenate(
        [updated[batch].astype(jnp.float32) for batch in range(batch_count)], axis=0
    )
    for expert in range(returned.shape[0]):
        total = total + weights[:, expert : expert + 1] * returned[expert].astype(jnp.float32)
    for batch in range(batch_count):
        out[batch] = total[batch * row_count : (batch + 1) * row_count].astype(jnp.bfloat16)


def combine(shares, updated, returned):
    return pl.pallas_call(
        combine_kernel,
        out_shape=jax.ShapeDtypeStruct(updated.shape, jnp.bfloat16),
        in_specs=[vmem_spec] * 3,
        out_specs=vmem_spec,
        compiler_params=pltpu.CompilerParams(vmem_limit_bytes=8 * mebibyte),
        name="combine",
    )(shares, updated, returned)


def body(
    queries,
    cache_keys,
    cache_values,
    new_keys,
    new_values,
    lengths,
    out_weight,
    residual,
    norm_gain,
    routes,
    route_probs,
    w_gate,
    w_up,
    w_down,
):
    side_count = lax.axis_size("side")
    dev_count = lax.axis_size("dev")
    batch_count, row_count, _, column_width = residual.shape
    rows = batch_count * row_count
    swap = [(0, 1), (1, 0)]

    attended, shares = attend(
        queries, cache_keys, cache_values, new_keys, new_values, lengths, routes, route_probs
    )
    if dev_count == 2:
        attended = (attended, lax.ppermute(attended, "dev", swap))
    else:
        attended = (lax.all_gather(attended, "dev", axis=0, tiled=True),)
    updated, copies = project(
        attended,
        out_weight,
        residual.reshape(batch_count, row_count, column_width),
        dev_count,
        side_count,
    )
    arrived = lax.all_to_all(copies, "side", split_axis=0, concat_axis=0, tiled=True)
    arrived = arrived.reshape(side_count * rows, column_width)
    gather_and_run = pair_experts if dev_count == 2 else whole_experts
    total = gather_and_run(arrived, norm_gain, w_gate[0], w_up[0], w_down[0])
    total = total.astype(jnp.bfloat16).reshape(side_count, rows, column_width)
    returned = lax.all_to_all(total, "side", split_axis=0, concat_axis=0, tiled=True)
    result = combine(shares, updated, returned)
    return result.reshape(residual.shape)


def solution(mesh):
    placed = (
        P("groups", "dev", "side", None, None),
        P("groups", "dev", "side", None, None, None),
        P("groups", "dev", "side", None, None, None),
        P("groups", "dev", "side", None, None),
        P("groups", "dev", "side", None, None),
        P("groups", "dev", "side"),
        P(None, "dev"),
        P("groups", None, "side", "dev"),
        P(),
        P("groups", None, None, None),
        P("groups", None, "side", None),
        P("side", "dev", None),
        P("side", "dev", None),
        P("side", "dev", None),
    )
    return jax.shard_map(
        body,
        mesh=mesh,
        in_specs=placed,
        out_specs=P("groups", None, "side", "dev"),
        check_vma=False,
    )
```

```python
import functools
import math

import jax
import jax.numpy as jnp
from jax import lax
from jax.experimental import pallas as pl
from jax.experimental.pallas import tpu as pltpu
from jax.sharding import PartitionSpec as P

norm_epsilon = 1e-05
mebibyte = 1024 * 1024
mxu_count, mxu_size = 2, 256
hint_flops = 40_000_000_000
last_last = (((1,), (1,)), ((), ()))

smem_spec = pl.BlockSpec(memory_space=pltpu.SMEM)
vmem_spec = pl.BlockSpec(memory_space=pltpu.VMEM)
in_hbm = functools.partial(pltpu.with_memory_space_constraint, memory_space=pltpu.HBM)
in_vmem = functools.partial(pltpu.with_memory_space_constraint, memory_space=pltpu.VMEM)


def share_rows(routes, probs, shares):
    batch_count, row_count, _ = shares.shape
    top_count = routes.shape[2]
    side_index = lax.axis_index("side")
    row_ids = lax.broadcasted_iota(jnp.int32, shares.shape[1:], 0)
    lane_ids = lax.broadcasted_iota(jnp.int32, shares.shape[1:], 1)
    for batch in range(batch_count):

        def place(row, placed):
            for top in range(top_count):
                expert = routes[batch, row, top, side_index]
                placed = jnp.where(
                    (row_ids == row) & (lane_ids == expert), probs[batch, row, 0, top], placed
                )
            return placed

        placed = jnp.zeros(shares.shape[1:], jnp.float32)
        if row_count <= 8:
            for row in range(row_count):
                placed = place(row, placed)
        else:
            placed = lax.fori_loop(0, row_count, place, placed)
        shares[batch] = placed / jnp.sum(placed, axis=-1, keepdims=True)


def attend_kernel(
    lengths, routes, probs, queries, keys, values, new_keys, new_values, out, shares, scratch
):
    row_count, head_count, head_width = queries.shape
    pair_count = keys.shape[1]
    key_heads = new_keys.shape[1]
    width = head_count // key_heads
    local_rows = lengths.shape[2]
    factor = 1.0 / math.sqrt(head_width)
    pair = lax.broadcasted_iota(jnp.int32, (head_count, pair_count), 1)
    head = lax.broadcasted_iota(jnp.int32, (head_count, pair_count), 0)
    own_key = (pair % key_heads) == (head // width)
    position = jnp.where(own_key, pair // key_heads, pair_count)
    key_head = lax.broadcasted_iota(jnp.int32, (head_count, head_width), 0) // width

    def spread(block):
        wide = block.astype(jnp.float32)
        result = jnp.zeros((head_count, head_width), jnp.float32)
        for index in range(key_heads):
            result = jnp.where(key_head == index, wide[index : index + 1, :], result)
        return result

    all_rows = range(row_count)
    scores = [
        lax.dot_general(queries[row], keys[row], last_last, preferred_element_type=jnp.float32)
        for row in all_rows
    ]
    fresh = [
        jnp.sum(queries[row].astype(jnp.float32) * spread(new_keys[row]), axis=-1, keepdims=True)
        for row in all_rows
    ]
    lengths_of = [lengths[row // local_rows, 0, row % local_rows] for row in all_rows]
    raised = [
        jnp.where(position < lengths_of[row], jnp.exp(scores[row] * factor), 0.0)
        for row in all_rows
    ]
    raised_new = [jnp.exp(fresh[row] * factor) for row in all_rows]
    inverse = [
        1.0 / (jnp.sum(raised[row], axis=-1, keepdims=True) + raised_new[row]) for row in all_rows
    ]
    mixed = [
        jnp.dot(
            (raised[row] * inverse[row]).astype(jnp.bfloat16),
            values[row],
            preferred_element_type=jnp.float32,
        )
        for row in all_rows
    ]
    for row in all_rows:
        weight_new = (raised_new[row] * inverse[row]).astype(jnp.bfloat16).astype(jnp.float32)
        scratch[pl.ds(row * head_count, head_count), :] = mixed[row] + weight_new * spread(
            new_values[row]
        )
    pieces = [
        scratch[pl.ds(index, row_count, stride=head_count), :] for index in range(head_count)
    ]
    out[...] = jnp.concatenate(pieces, axis=1).astype(jnp.bfloat16)
    share_rows(routes, probs, shares)


def attend(queries, cache_keys, cache_values, new_keys, new_values, lengths, routes, probs):
    batch_count, local_rows = queries.shape[:2]
    rows = batch_count * local_rows
    head_count, head_width = queries.shape[-2:]
    key_heads = cache_keys.shape[-2]
    pairs = cache_keys.shape[-3] * key_heads
    return pl.pallas_call(
        attend_kernel,
        out_shape=(
            jax.ShapeDtypeStruct((rows, head_count * head_width), jnp.bfloat16),
            jax.ShapeDtypeStruct((batch_count, routes.shape[1], 128), jnp.float32),
        ),
        in_specs=[smem_spec] * 3 + [vmem_spec] * 5,
        out_specs=(vmem_spec, vmem_spec),
        scratch_shapes=[pltpu.VMEM((rows * head_count, head_width), jnp.float32)],
        compiler_params=pltpu.CompilerParams(vmem_limit_bytes=50 * mebibyte),
        name="attend",
        cost_estimate=pl.CostEstimate(
            flops=8_000_000_000, transcendentals=0, bytes_accessed=cache_keys.size * 4
        ),
    )(
        in_hbm(jnp.swapaxes(lengths, 1, 2)),
        in_hbm(jnp.swapaxes(routes, 2, 3)),
        in_hbm(probs),
        in_hbm(queries.reshape(rows, head_count, head_width)),
        in_hbm(cache_keys.reshape(rows, pairs, head_width)),
        in_hbm(cache_values.reshape(rows, pairs, head_width)),
        in_hbm(new_keys.reshape(rows, key_heads, head_width)),
        in_hbm(new_values.reshape(rows, key_heads, head_width)),
    )


def halves(dev_index, own, other):
    first = jnp.where(dev_index == 0, own, other)
    second = jnp.where(dev_index == 0, other, own)
    return first, second


def project_kernel(dev_count, *refs):
    attended, (out_weight, residual, updated, copies) = refs[:-4], refs[-4:]
    batch_count, row_count, _ = residual.shape
    local_rows = row_count // dev_count
    parts = [ref[...] for ref in attended]
    if len(parts) == 2:
        parts = [part.astype(jnp.float32) for part in parts]
        rows = jnp.concatenate(halves(lax.axis_index("dev"), *parts), axis=0).astype(jnp.bfloat16)
    else:
        rows = parts[0]
    result = jnp.dot(rows, out_weight[...], preferred_element_type=jnp.float32)
    whole = []
    for batch in range(batch_count):
        pieces = []
        for dev in range(dev_count):
            start = (dev * batch_count + batch) * local_rows
            pieces.append(result[start : start + local_rows, :])
        projected = jnp.concatenate(pieces, axis=0).astype(jnp.bfloat16)
        rows = (residual[batch].astype(jnp.float32) + projected.astype(jnp.float32)).astype(
            jnp.bfloat16
        )
        updated[batch] = rows
        whole.append(rows.astype(jnp.float32))
    whole = jnp.concatenate(whole, axis=0).astype(jnp.bfloat16)
    for side in range(copies.shape[0]):
        copies[side] = whole


def project(attended, out_weight, residual, dev_count, side_count):
    batch_count, row_count, width = residual.shape
    rows = batch_count * row_count
    return pl.pallas_call(
        functools.partial(project_kernel, dev_count),
        out_shape=(
            jax.ShapeDtypeStruct((batch_count, row_count, width), jnp.bfloat16),
            jax.ShapeDtypeStruct((side_count, rows, width), jnp.bfloat16),
        ),
        in_specs=[vmem_spec] * (len(attended) + 2),
        out_specs=(vmem_spec, vmem_spec),
        compiler_params=pltpu.CompilerParams(vmem_limit_bytes=2 * mebibyte),
        cost_estimate=pl.CostEstimate(
            flops=hint_flops, transcendentals=0, bytes_accessed=out_weight.size * 2
        ),
        name="project",
    )(*attended, in_vmem(out_weight), residual)


def pieces_of(length, piece):
    return [(start, min(piece, length - start)) for start in range(0, length, piece)]


def normalize(parts, gain):
    width = sum(part.shape[1] for part in parts)
    center = sum(jnp.sum(part, axis=-1, keepdims=True) for part in parts) / width
    parts = [part - center for part in parts]
    spread = sum(jnp.sum(jnp.square(part), axis=-1, keepdims=True) for part in parts) / width
    values = jnp.concatenate(parts, axis=1) if len(parts) > 1 else parts[0]
    return values * lax.rsqrt(spread + norm_epsilon) * gain


def hidden_rows(parts, gain, w_gate, w_up, hidden):
    rows = normalize(parts, gain[...]).astype(jnp.bfloat16)
    for start, size in pieces_of(w_gate.shape[0], 896):
        span = slice(start, start + size)
        gate = lax.dot_general(w_gate[span, :], rows, last_last, preferred_element_type=jnp.float32)
        up = lax.dot_general(w_up[span, :], rows, last_last, preferred_element_type=jnp.float32)
        hidden[:, span] = (gate / (1.0 + jnp.exp(-gate)) * up).T.astype(jnp.bfloat16)


def mixed_plan(units, inner):
    own = units // mxu_count
    blocks = own // mxu_size
    rest = own - blocks * mxu_size
    return own, blocks, rest, (own + rest) // 2, inner // mxu_size


def mixed_products(normed, turned, w_gate, w_up, hidden, held, *sums):
    units, inner = w_gate.shape
    row_count = normed.shape[0]
    own, blocks, rest, streamed, depth = mixed_plan(units, inner)
    wide, narrow = sums[:mxu_count], sums[mxu_count:]

    def piece(index):
        return slice(index * mxu_size, (index + 1) * mxu_size)

    def finish(block):
        for unit in range(mxu_count):
            start = unit * own + block * mxu_size
            up = pltpu.matmul_pop(narrow[unit * blocks + block])
            gate = held[start : start + mxu_size, :].T[:row_count]
            hidden[:, start : start + mxu_size] = (gate / (1.0 + jnp.exp(-gate)) * up).astype(
                jnp.bfloat16
            )

    finished = 0
    for turn in range(2):
        loaded = [(block, k) for block in range(blocks) for k in range(depth)]
        middle = (len(loaded) + 1) // 2
        loaded = loaded[:middle] if turn == 0 else loaded[middle:]
        steps, done = [], 0
        for k in range(depth):
            upto = (k + 1) * len(loaded) // depth
            steps += loaded[done : done + 1] + [(None, k)] + loaded[done + 1 : upto]
            done = upto

        def load(index, unit):
            block, k = steps[index]
            if block is None:
                pltpu.matmul_push_rhs(turned[piece(k), :], index % 2, unit)
            else:
                start = unit * own + block * mxu_size
                tile = w_up[start : start + mxu_size, piece(k)]
                pltpu.matmul_push_rhs(tile, index % 2, unit, transpose=True)

        def multiply(index, unit):
            block, k = steps[index]
            start, stop = unit * own, (unit + 1) * own
            if block is not None:
                target, left = narrow[unit * blocks + block], normed[:, piece(k)]
            elif turn == 0:
                target, left = wide[unit], w_gate[start : start + streamed, piece(k)]
            else:
                target, left = wide[unit], w_gate[start + streamed : stop, piece(k)]
                if rest:
                    left = jnp.concatenate([left, w_up[stop - rest : stop, piece(k)]], axis=0)
            pltpu.matmul_acc_lhs(target, left, load_staged_rhs=index % 2)

        for unit in range(mxu_count):
            load(0, unit)
            load(1, unit)
        for index in range(len(steps)):
            for unit in range(mxu_count):
                multiply(index, unit)
                if index + 2 < len(steps):
                    load(index + 2, unit)
        for unit in range(mxu_count):
            result = pltpu.matmul_pop(wide[unit])[:, :128]
            start = unit * own
            if turn == 0:
                held[start : start + streamed, :] = result
            else:
                held[start + streamed : start + own, :] = result[: own - streamed]
                if rest:
                    held[units + unit * rest : units + (unit + 1) * rest, :] = result[
                        own - streamed :
                    ]

        ready = blocks if turn else min(middle // depth, streamed // mxu_size)
        for block in range(finished, ready):
            finish(block)
        finished = ready

    for unit in range(mxu_count):
        if rest:
            start = unit * own + blocks * mxu_size
            gate = held[start : start + rest, :]
            up = held[units + unit * rest : units + (unit + 1) * rest, :]
            value = (gate / (1.0 + jnp.exp(-gate)) * up).T[:row_count]
            hidden[:, start : start + rest] = value.astype(jnp.bfloat16)


def loaded_products(hidden, weight, out, *sums):
    row_count, inner = hidden.shape
    blocks = out.shape[1] // mxu_size // mxu_count
    starts = list(range(0, inner - mxu_size + 1, mxu_size))
    left = inner - starts[-1] - mxu_size
    lefts = [hidden[:, start : start + mxu_size] for start in starts]
    if left:
        starts.append(inner - mxu_size)
        zeros = jnp.zeros((row_count, mxu_size - left), jnp.bfloat16)
        lefts.append(jnp.concatenate([zeros, hidden[:, inner - left :]], axis=1))
    steps = [(block, k) for block in range(blocks) for k in range(len(starts))]

    def load(index, unit):
        block, k = steps[index]
        column = (unit * blocks + block) * mxu_size
        tile = weight[starts[k] : starts[k] + mxu_size, column : column + mxu_size]
        pltpu.matmul_push_rhs(tile, index % 2, unit)

    for unit in range(mxu_count):
        load(0, unit)
        load(1, unit)
    for index, (block, k) in enumerate(steps):
        for unit in range(mxu_count):
            pltpu.matmul_acc_lhs(
                sums[unit * blocks + block], lefts[k], load_staged_rhs=index % 2
            )
            if index + 2 < len(steps):
                load(index + 2, unit)
        if k == len(starts) - 1:
            for unit in range(mxu_count):
                column = (unit * blocks + block) * mxu_size
                result = pltpu.matmul_pop(sums[unit * blocks + block])
                out[:, column : column + mxu_size] = result.astype(jnp.bfloat16)


def pair_kernel(own, other, gain, w_gate, w_up, w_down, hidden, given, kept, *scratch):
    lent, normed, turned, held, arrived = scratch
    dev_index = lax.axis_index("dev")
    row_count, width = own.shape
    units, inner = w_gate.shape
    copies = [
        pltpu.make_async_copy(
            w_down.at[:, pl.ds(pl.multiple_of(dev * width, width), width)],
            target,
            arrived.at[index],
        )
        for index, (dev, target) in enumerate(((1 - dev_index, lent), (dev_index, kept)))
    ]
    for copy in copies:
        copy.start()

    @pl.when(dev_index < 2)
    def _():
        parts = halves(dev_index, own[...].astype(jnp.float32), other[...].astype(jnp.float32))
        rows = normalize(parts, gain[...])
        normed[...] = rows.astype(jnp.bfloat16)
        columns = rows.T.astype(jnp.bfloat16)
        turned[:, :128] = jnp.concatenate(
            [columns, jnp.zeros((inner, 128 - row_count), jnp.bfloat16)], axis=1
        )
        turned[:, 128:] = jnp.zeros((inner, mxu_size - 128), jnp.bfloat16)
        _, blocks, _, streamed, _ = mixed_plan(units, inner)
        sums = [pltpu.ACC(unit)((streamed, mxu_size), jnp.float32) for unit in range(mxu_count)]
        for unit in range(mxu_count):
            sums += [pltpu.ACC(unit)((row_count, mxu_size), jnp.float32)] * blocks
        pl.run_scoped(
            functools.partial(mixed_products, normed, turned, w_gate, w_up, hidden, held), *sums
        )

    for copy in copies:
        copy.wait()
    blocks = width // mxu_size // mxu_count
    sums = [
        pltpu.ACC(unit)((row_count, mxu_size), jnp.float32)
        for unit in range(mxu_count)
        for _ in range(blocks)
    ]
    pl.run_scoped(functools.partial(loaded_products, hidden, lent, given), *sums)


def down_kernel(hidden, kept, out):
    out[...] = jnp.dot(hidden[...], kept[...], preferred_element_type=jnp.float32).astype(
        jnp.bfloat16
    )


def pair_experts(arrived, gain, w_gate, w_up, w_down):
    swap = [(0, 1), (1, 0)]
    rows, half = arrived.shape
    units, width = w_gate.shape
    hidden, given, kept = pl.pallas_call(
        pair_kernel,
        out_shape=(
            jax.ShapeDtypeStruct((rows, units), jnp.bfloat16),
            jax.ShapeDtypeStruct((rows, half), jnp.bfloat16),
            pltpu.VMEM((units, half), jnp.bfloat16),
        ),
        in_specs=[vmem_spec] * 5 + [pl.BlockSpec(memory_space=pl.ANY)],
        out_specs=(vmem_spec,) * 3,
        scratch_shapes=[
            pltpu.VMEM((units, half), jnp.bfloat16),
            pltpu.VMEM((rows, width), jnp.bfloat16),
            pltpu.VMEM((width, mxu_size), jnp.bfloat16),
            pltpu.VMEM((units + mxu_count * mxu_size, 128), jnp.float32),
            pltpu.SemaphoreType.DMA((2,)),
        ],
        compiler_params=pltpu.CompilerParams(vmem_limit_bytes=12 * mebibyte),
        name="experts",
    )(
        arrived,
        lax.ppermute(arrived, "dev", swap),
        gain.reshape(1, width),
        in_vmem(w_gate),
        in_vmem(w_up),
        in_hbm(w_down),
    )
    taken = lax.ppermute(given, "dev", swap)
    own = pl.pallas_call(
        down_kernel,
        out_shape=jax.ShapeDtypeStruct((rows, half), jnp.bfloat16),
        in_specs=[vmem_spec, vmem_spec],
        out_specs=vmem_spec,
        compiler_params=pltpu.CompilerParams(vmem_limit_bytes=2 * mebibyte),
        name="down_own",
    )(hidden, in_vmem(kept))
    return own.astype(jnp.float32) + taken.astype(jnp.float32)


def whole_kernel(rows, gain, w_gate, w_up, w_down, out, hidden):
    hidden_rows([rows[...].astype(jnp.float32)], gain, w_gate, w_up, hidden)
    out[...] = jnp.dot(hidden[...], w_down[...], preferred_element_type=jnp.float32).astype(
        jnp.bfloat16
    )


def whole_experts(arrived, gain, w_gate, w_up, w_down):
    rows, part_width = arrived.shape
    units, width = w_gate.shape
    block = min(rows, 128)
    gathered = lax.all_gather(arrived, "dev", axis=1, tiled=True)
    given = pl.pallas_call(
        whole_kernel,
        grid=(rows // block,),
        out_shape=jax.ShapeDtypeStruct((rows, width), jnp.bfloat16),
        in_specs=[pl.BlockSpec((block, width), lambda r: (r, 0))]
        + [pl.BlockSpec((1, width), lambda r: (0, 0)), vmem_spec, vmem_spec, vmem_spec],
        out_specs=pl.BlockSpec((block, width), lambda r: (r, 0)),
        scratch_shapes=[pltpu.VMEM((block, units), jnp.bfloat16)],
        compiler_params=pltpu.CompilerParams(vmem_limit_bytes=24 * mebibyte),
        name="experts",
    )(gathered, gain.reshape(1, width), w_gate, w_up, w_down)
    pieces = given.reshape(rows, width // part_width, part_width)
    pieces = lax.all_to_all(pieces, "dev", split_axis=1, concat_axis=1, tiled=True)
    return jnp.sum(pieces.astype(jnp.float32), axis=1)


def combine_kernel(shares, updated, returned, out):
    batch_count, row_count, _ = updated.shape
    weights = jnp.concatenate([shares[batch] for batch in range(batch_count)], axis=0)
    total = jnp.concatenate(
        [updated[batch].astype(jnp.float32) for batch in range(batch_count)], axis=0
    )
    for expert in range(returned.shape[0]):
        total = total + weights[:, expert : expert + 1] * returned[expert].astype(jnp.float32)
    for batch in range(batch_count):
        out[batch] = total[batch * row_count : (batch + 1) * row_count].astype(jnp.bfloat16)


def combine(shares, updated, returned):
    return pl.pallas_call(
        combine_kernel,
        out_shape=jax.ShapeDtypeStruct(updated.shape, jnp.bfloat16),
        in_specs=[vmem_spec] * 3,
        out_specs=vmem_spec,
        compiler_params=pltpu.CompilerParams(vmem_limit_bytes=8 * mebibyte),
        name="combine",
    )(shares, updated, returned)


def body(
    queries,
    cache_keys,
    cache_values,
    new_keys,
    new_values,
    lengths,
    out_weight,
    residual,
    norm_gain,
    routes,
    route_probs,
    w_gate,
    w_up,
    w_down,
):
    side_count = lax.axis_size("side")
    dev_count = lax.axis_size("dev")
    batch_count, row_count, _, column_width = residual.shape
    rows = batch_count * row_count
    swap = [(0, 1), (1, 0)]

    attended, shares = attend(
        queries, cache_keys, cache_values, new_keys, new_values, lengths, routes, route_probs
    )
    if dev_count == 2:
        attended = (attended, lax.ppermute(attended, "dev", swap))
    else:
        attended = (lax.all_gather(attended, "dev", axis=0, tiled=True),)
    updated, copies = project(
        attended,
        out_weight,
        residual.reshape(batch_count, row_count, column_width),
        dev_count,
        side_count,
    )
    arrived = lax.all_to_all(copies, "side", split_axis=0, concat_axis=0, tiled=True)
    arrived = arrived.reshape(side_count * rows, column_width)
    gather_and_run = pair_experts if dev_count == 2 else whole_experts
    total = gather_and_run(arrived, norm_gain, w_gate[0], w_up[0], w_down[0])
    total = total.astype(jnp.bfloat16).reshape(side_count, rows, column_width)
    returned = lax.all_to_all(total, "side", split_axis=0, concat_axis=0, tiled=True)
    result = combine(shares, updated, returned)
    return result.reshape(residual.shape)


def solution(mesh):
    placed = (
        P("groups", "dev", "side", None, None),
        P("groups", "dev", "side", None, None, None),
        P("groups", "dev", "side", None, None, None),
        P("groups", "dev", "side", None, None),
        P("groups", "dev", "side", None, None),
        P("groups", "dev", "side"),
        P(None, "dev"),
        P("groups", None, "side", "dev"),
        P(),
        P("groups", None, None, None),
        P("groups", None, "side", None),
        P("side", "dev", None),
        P("side", "dev", None),
        P("side", "dev", None),
    )
    return jax.shard_map(
        body,
        mesh=mesh,
        in_specs=placed,
        out_specs=P("groups", None, "side", "dev"),
        check_vma=False,
    )
```
